32 devices in a mesh: sect: 4 (over y, x), dom: 8 (over z, core).
Axes of the slice: x: 2, y: 2, z: 4, core: 2. Of those that a mesh axis runs over, the one named last changes fastest.
Arguments:
- fluid_source: float32 [4096, 32, 128], P(('sect', 'dom')), may hold values from -8 to 8
- coef_ids: int32 [4096, 32, 128], P(('sect', 'dom')), may hold values from 0 to 15
- coef_table: float32 [16], replicated, may hold values from 0.5 to 8
- owner_device: int32 [4096, 1], P(('sect', 'dom')), may hold values from 0 to 31; in each aligned block of 128 rows (0 to 127, 128 to 255, ...) at most 8 rows name the same one
- owner_slot: int32 [4096, 1], P(('sect', 'dom')), may hold values from 0 to 127
- solid_init: float32 [4096, 128], P(('sect', 'dom')), may hold values from -4 to 4
- solid_load: float32 [4096, 128], P(('sect', 'dom')), may hold values from -6 to 6
- compliance: float32 [128, 128], replicated, may hold values from -0.5 to 0.5
Outputs:
- fluid_state: float32 [4096, 32, 128], P(('sect', 'dom'))
- displacement: float32 [4096, 128], P(('sect', 'dom'))
- coupling_norms: float32 [2], replicated
The draws below stay inside these ranges and needn't reach their ends.
Inputs may be any that keep to these rules, and one draw needn't show every extreme that they name: `owner_device`: among the 128 rows of one device no owner device is named more than 8 times, a bound that some block reaches.
All inputs are finite; a program needn't handle non-finite values.
Results may differ from the reference program's by a relative error of at most 0.0001.
Values sent between devices are 32-bit elements; how exact they have to be, the bound alone decides.
A program may use at most 64 MiB of HBM per device.

```python
import math
import jax
import jax.numpy as jnp
import numpy as np
from jax import lax

ROW = 128
FX = 128
FY = 32
SDEV = 128
NCOEF = 16
SWEEPS = 3
COUPLE = 2
CAP = 8
NXF = 4096
NS = 4096
DEVICES = 32


def set_ends(array, rng, smallest, high):
    index_at = [jax.random.randint(jax.random.fold_in(rng, axis), (), 0, length) for axis, length in enumerate(array.shape)]
    main_axis = array.shape.index(max(array.shape))
    beside = index_at[:main_axis] + [(index_at[main_axis] + 1) % array.shape[main_axis]] + index_at[main_axis + 1:]
    return array.at[tuple(index_at)].set(smallest).at[tuple(beside)].set(high)


def shard_levels(rng, dims, shards, low, high):
    def one(position, parts):
        draws = jax.random.uniform(jax.random.fold_in(jax.random.fold_in(rng, 6), position), (parts,), jnp.float32, low / len(shards), high / len(shards))
        return jnp.repeat(jnp.exp(draws), dims[position] // parts).reshape((-1,) + (1,) * (len(dims) - position - 1))

    loudness = one(*shards[0])
    for cut in shards[1:]:
        loudness = loudness * one(*cut)
    return loudness


def routed_block(key, own, number, rows, amount, top, reach, skew):
    order = jax.random.permutation(key, amount)
    crowded, ordinary = portions_of(amount, rows * top, reach, skew, True), portions_of(amount, rows * top, reach, skew, False)
    places = jnp.arange(amount)

    def named(tallies, turn):
        used = int((tallies > 0).sum())
        fixed = max(1, used // 4)
        moved = fixed + (places - fixed + turn * (used - fixed)) % max(1, amount - fixed)
        return jnp.zeros((amount,), jnp.int32).at[order[jnp.where(places < fixed, places, moved)]].set(jnp.asarray(tallies, jnp.int32))

    tallies = jnp.where(number % 4 == 0, named(crowded, number // 4), named(ordinary, number - number // 4 - 1))
    mixed = jax.random.permutation(jax.random.fold_in(own, 3), amount)
    giver, sink = mixed[0:amount // 2 * 2:2], mixed[1:amount // 2 * 2:2]
    slack = jnp.minimum(tallies[giver] - 1, reach - tallies[sink]) // 2
    slack = jnp.where((giver == order[0]) | (sink == order[0]) | (tallies[sink] == 0), 0, jnp.maximum(slack, 0))
    moved = jax.random.randint(jax.random.fold_in(own, 4), (amount // 2,), 0, 1 << 20) % (slack + 1)
    tallies = tallies.at[giver].add(-moved).at[sink].add(moved)
    labels = jnp.searchsorted(jnp.cumsum(tallies), jnp.arange(rows * top), side="right").astype(jnp.int32)
    grid = labels.reshape(top, rows).T
    grid = grid[jax.random.permutation(jax.random.fold_in(own, 1), rows)]
    turn = jax.random.randint(jax.random.fold_in(own, 2), (rows, 1), 0, top)
    return jnp.take_along_axis(grid, (jnp.arange(top)[None, :] + turn) % top, axis=1)


def portions_of(count, total, reach, skew, full):
    loads = [(1 << 20) // math.isqrt(grade ** skew) + 1 for grade in range(1, count + 1)]
    largest = reach if full else min(reach, max(-(-total // count), total * loads[0] // sum(loads)))
    least = 1 if total - largest >= count - 1 else 0
    given, rest = [largest] + [least] * (count - 1), total - largest - least * (count - 1)
    while rest > 0:
        free = [i for i in range(1, count) if given[i] < largest] or [i for i in range(1, count) if given[i] < reach]
        mass, remaining = sum([loads[i] for i in free]), rest
        for i in free:
            more = min(reach - given[i], max(1, remaining * loads[i] // mass), rest)
            given[i] = given[i] + more
            rest = rest - more
    return np.array(given)


def normal_values(key, extent, width, bound, split=(), held_as=jnp.bfloat16):
    factor_of = shard_levels(key, extent, split, -0.22, 0.18) if split else 1.0
    entries = jax.random.normal(key, extent, jnp.float32) * width * factor_of
    return jnp.minimum(jnp.maximum(entries, -bound), bound).astype(held_as)


def setup_inputs(seed: int = 0) -> dict:
    arg_keys = jax.random.split(jax.random.key(seed), 9)
    fluid_source = normal_values(arg_keys[0], (NXF, FY, ROW), 1.0, 8.0, ((0, 32),), jnp.float32)
    coef_ids = set_ends(jax.random.randint(arg_keys[1], (NXF, FY, ROW), 0, NCOEF), jax.random.fold_in(arg_keys[1], 1), 0, NCOEF - 1).astype(jnp.int32)
    coef_table = jnp.clip(jnp.exp(jax.random.uniform(arg_keys[2], (NCOEF,), jnp.float32, math.log(0.5), math.log(8.0))), 0.5, 8.0)
    owner_device_keys = jax.random.split(jax.random.fold_in(arg_keys[3], 1), NXF // FX)
    owner_device_turns = jax.random.permutation(jax.random.fold_in(arg_keys[3], 3), NXF // FX)
    owner_device = jax.vmap(lambda own, number: routed_block(jax.random.fold_in(arg_keys[3], 2), own, number, FX, DEVICES, 1, CAP, 2))(owner_device_keys, owner_device_turns).reshape((NXF, 1))
    owner_slot = set_ends(jax.random.randint(arg_keys[4], (NXF, 1), 0, SDEV), jax.random.fold_in(arg_keys[4], 1), 0, SDEV - 1).astype(jnp.int32)
    solid_init = normal_values(arg_keys[5], (NS, ROW), 0.5, 4.0, ((0, 32),), jnp.float32)
    solid_load = normal_values(arg_keys[6], (NS, ROW), 1.0, 6.0, ((0, 32),), jnp.float32)
    compliance = normal_values(arg_keys[7], (ROW, ROW), ROW ** -0.5, 0.5, (), jnp.float32)
    return dict(fluid_source=fluid_source, coef_ids=coef_ids, coef_table=coef_table, owner_device=owner_device, owner_slot=owner_slot, solid_init=solid_init, solid_load=solid_load, compliance=compliance)


def neighbours(fluid_state):
    padded = jnp.pad(fluid_state, 1)
    total = padded[2:, 1:-1, 1:-1] + padded[:-2, 1:-1, 1:-1]
    total = total + padded[1:-1, 2:, 1:-1] + padded[1:-1, :-2, 1:-1]
    total = total + padded[1:-1, 1:-1, 2:] + padded[1:-1, 1:-1, :-2]
    return total

def reference(fluid_source, coef_ids, coef_table, owner_device, owner_slot, solid_init, solid_load, compliance):
    diagonal = 6.0 + coef_table[coef_ids]
    target_row = (owner_device[:, 0] * SDEV + owner_slot[:, 0]).astype(jnp.int32)
    fluid_state = jnp.zeros(fluid_source.shape, jnp.float32)
    displacement = solid_init
    norm_list = []
    for iteration in range(COUPLE):
        wall_rows = displacement[target_row]
        source = fluid_source.at[:, 0, :].add(wall_rows)
        for sweep_index in range(SWEEPS):
            fluid_state = (source + neighbours(fluid_state)) / diagonal
        traction = fluid_state[:, 0, :] - fluid_state[:, 1, :]
        solid_force = jax.ops.segment_sum(traction, target_row, num_segments=NS) + solid_load
        trial_disp = jnp.dot(solid_force, compliance, precision=lax.Precision.HIGHEST)
        mismatch = trial_disp - displacement
        norm_list.append(jnp.sqrt(jnp.sum(mismatch * mismatch) + 1e-06))
        displacement = displacement + 0.5 * mismatch
    return (fluid_state, displacement, jnp.stack(norm_list))
```

```python
import functools

import jax
import jax.numpy as jnp
from jax import lax
from jax.experimental import pallas as pl
from jax.experimental.pallas import tpu as pltpu
from jax.sharding import PartitionSpec as P

SWEEPS = 3
COUPLE = 2
RELAX = 0.5
TOTAL = SWEEPS * COUPLE
GHOST = TOTAL - 1
PAD = 8
MESH = pl.DeviceIdType.MESH


def iota(shape, dim):
    return lax.broadcasted_iota(jnp.int32, shape, dim)


def pieces(x):
    high = x.astype(jnp.bfloat16)
    low = (x - high.astype(jnp.float32)).astype(jnp.bfloat16)
    return high, low


def pick(onehot, x):
    width = x.shape[1]
    both = jnp.concatenate(pieces(x), axis=1)
    out = jnp.dot(onehot, both, preferred_element_type=jnp.float32)
    return out[:, :width] + out[:, width:]


def product(x, y):
    xh, xl = pieces(x)
    yh, yl = pieces(y)
    left = jnp.concatenate([xh, xh, xl], axis=1)
    right = jnp.concatenate([yh, yl, yh], axis=0)
    return jnp.dot(left, right, preferred_element_type=jnp.float32)


def beside(x):
    rows, width = x.shape
    lane = iota(x.shape, 1)
    low = jnp.where(lane == 0, 0.0, pltpu.roll(x, 1, 1))
    high = jnp.where(lane == width - 1, 0.0, pltpu.roll(x, width - 1, 1))
    return low + high


def kernel(
    n, dom, source, ids, table, owner, slot, init, load, compliance,
    state_out, disp_out, norm_out,
    src, idv, inv, even, odd, invp, base, walls, force,
    place, place_t, choose, choose_t,
    req_s, req_r, wall_s, wall_r, trac_s, trac_r, norm_s, norm_r,
    in_sem, out_sem, ghost_ss, ghost_rs, a2a_ss, a2a_rs, edge_ss, edge_rs,
):
    rows, depth, width = source.shape
    end = PAD + rows
    cap = PAD
    me = lax.axis_index("sect") * dom + lax.axis_index("dom")

    def coords(index):
        return (lax.div(index, dom), lax.rem(index, dom))

    right = coords(lax.rem(me + 1, n))
    left = coords(lax.rem(me + n - 1, n))

    loads = [
        pltpu.make_async_copy(source, src.at[pl.ds(PAD, rows)], in_sem.at[0]),
        pltpu.make_async_copy(ids, idv.at[pl.ds(PAD, rows)], in_sem.at[1]),
    ]
    for copy in loads:
        copy.start()

    barrier = pltpu.get_barrier_semaphore()

    def greet(k, carry):
        pl.semaphore_signal(
            barrier, inc=1, device_id=coords(lax.rem(me + k, n)), device_id_type=MESH
        )
        return carry

    lax.fori_loop(1, n, greet, 0)

    owner_row = owner[...]
    slot_row = slot[...]
    hits = (iota((n, rows), 0) == owner_row).astype(jnp.float32)
    before = (iota((rows, rows), 0) < iota((rows, rows), 1)).astype(jnp.bfloat16)
    earlier = jnp.dot(hits.astype(jnp.bfloat16), before, preferred_element_type=jnp.float32)
    rank = jnp.sum(earlier * hits, axis=0, keepdims=True).astype(jnp.int32)
    position = owner_row * cap + rank
    placed = (iota((n * cap, rows), 0) == position).astype(jnp.float32)
    place[...] = placed.astype(jnp.bfloat16)
    place_t[...] = placed.T.astype(jnp.bfloat16)
    wanted = jnp.sum(placed * (slot_row + 1).astype(jnp.float32), axis=1, keepdims=True) - 1.0
    wanted = wanted.reshape(n, cap, 1)
    square = iota((n, cap, width), 2) == iota((n, cap, width), 1)
    req_s[...] = jnp.sum(jnp.where(square, wanted, 0.0), axis=1, keepdims=True).astype(jnp.int32)

    pl.semaphore_wait(barrier, n - 1)

    def exchange(sent, got, phase):
        def one(k, carry):
            peer = lax.rem(me + k, n)
            pltpu.make_async_remote_copy(
                src_ref=sent.at[peer],
                dst_ref=got.at[me],
                send_sem=a2a_ss.at[phase],
                recv_sem=a2a_rs.at[phase],
                device_id=coords(peer),
                device_id_type=MESH,
            ).start()
            return carry

        lax.fori_loop(1, n, one, 0)
        got[me] = sent[me]

    def finish(ref, sem):
        part = ref.at[pl.ds(0, n - 1)]
        pltpu.make_async_copy(part, part, sem).wait()

    exchange(req_s, req_r, 0)

    def to_neighbours(from_low, from_high, to_low, to_high, ss, rs):
        copies = [
            pltpu.make_async_remote_copy(
                src_ref=a, dst_ref=b, send_sem=ss(i), recv_sem=rs(i),
                device_id=device, device_id_type=MESH,
            )
            for i, (a, b, device) in enumerate(
                ((from_low, to_high, left), (from_high, to_low, right))
            )
        ]
        for copy in copies:
            copy.start()
        return copies

    ghosts = []
    for number, (whole, held) in enumerate(((source, src), (ids, idv))):
        ghosts += to_neighbours(
            whole.at[pl.ds(0, GHOST)], whole.at[pl.ds(rows - GHOST, GHOST)],
            held.at[pl.ds(PAD - GHOST, GHOST)], held.at[pl.ds(end, GHOST)],
            lambda i: ghost_ss.at[number, i], lambda i: ghost_rs.at[number, i],
        )

    lane = iota((depth, width), 1)
    recip = jnp.zeros((depth, width), jnp.float32)
    for entry in range(table.shape[0]):
        recip = jnp.where(lane == entry, table[entry], recip)
    recip = 1.0 / (6.0 + recip)

    def first(x, scale):
        value = jnp.take_along_axis(recip, idv[x], axis=1, mode="promise_in_bounds")
        if scale is not None:
            value = value * scale
        inv[x] = value
        even[x] = src[x] * value

    for copy in loads:
        copy.wait()

    def first_block(i, carry):
        for j in range(4):
            first(PAD + 4 * i + j, None)
        return carry

    lax.fori_loop(0, rows // 4, first_block, 0)
    for x in list(range(PAD - GHOST)) + list(range(end + GHOST, end + PAD)):
        inv[x] = jnp.zeros((depth, width), jnp.float32)

    finish(req_r, a2a_rs.at[0])
    slots = jnp.sum(jnp.where(square, req_r[...].astype(jnp.float32), 0.0), axis=2, keepdims=True)
    chosen = (iota((n, cap, init.shape[0]), 2).astype(jnp.float32) == slots).astype(jnp.float32)
    chosen = chosen.reshape(n * cap, init.shape[0])
    choose[...] = chosen.astype(jnp.bfloat16)
    choose_t[...] = chosen.T.astype(jnp.bfloat16)

    wall_s[0] = pick(choose[...], init[...]).reshape(n, cap, width)
    exchange(wall_s.at[0], wall_r.at[0], 1)

    for copy in ghosts:
        copy.wait_recv()
    low_scale = jnp.where(me == 0, 0.0, 1.0)
    high_scale = jnp.where(me == n - 1, 0.0, 1.0)
    for x in range(GHOST):
        first(PAD - GHOST + x, low_scale)
        first(end + x, high_scale)
    for y in range(TOTAL):
        invp[y] = inv[:, y, :]

    row = iota((depth, width), 0)

    def sweep(number):
        old, new = (even, odd) if number % 2 == 1 else (odd, even)
        begin = PAD - (GHOST - number)
        count = rows + 2 * (GHOST - number)

        def planes(x, many):
            held = [old[x - 1 + j] for j in range(many + 2)]
            for j in range(many):
                here = held[j + 1]
                total = src[x + j] + (held[j] + held[j + 2])
                up = jnp.where(row == 0, 0.0, pltpu.roll(here, 1, 0))
                down = jnp.where(row == depth - 1, 0.0, pltpu.roll(here, depth - 1, 0))
                total = total + (up + down) + beside(here)
                new[x + j] = total * inv[x + j]

        def block(i, carry):
            planes(begin + 4 * i, 4)
            return carry

        lax.fori_loop(0, count // 4, block, 0)
        if count % 4:
            planes(begin + count // 4 * 4, count % 4)
        if number % SWEEPS == SWEEPS - 1:
            base[number // SWEEPS] = (
                new[PAD:end, 0, :] - new[PAD:end, 1, :]
            )

    def wall_of(k):
        finish(wall_r.at[k], a2a_rs.at[1 + 2 * k])
        got = wall_r[k].reshape(n * cap, width)
        walls[k, PAD:end, :] = pick(place_t[...], got)
        held = walls.at[k]
        return to_neighbours(
            held.at[pl.ds(PAD, PAD)], held.at[pl.ds(rows, PAD)],
            held.at[pl.ds(0, PAD)], held.at[pl.ds(end, PAD)],
            lambda i: edge_ss.at[k, i], lambda i: edge_rs.at[k, i],
        )

    def change(k, carried):
        wall = walls[k]
        total_rows = wall.shape[0]
        for _ in range(SWEEPS):
            after = []
            for y in range(len(carried) + 1):
                total = wall if y == 0 else None
                terms = []
                if y < len(carried):
                    here = carried[y]
                    terms += [
                        pltpu.roll(here, 1, 0) + pltpu.roll(here, total_rows - 1, 0),
                        beside(here),
                    ]
                if y > 0:
                    terms.append(carried[y - 1])
                if y + 1 < len(carried):
                    terms.append(carried[y + 1])
                for term in terms:
                    total = term if total is None else total + term
                after.append(total * invp[y])
            carried = after
        return carried

    def send_traction(k, carried):
        traction = base[k] + (carried[0] - carried[1])[PAD:end, :]
        trac_s[k] = pick(place[...], traction).reshape(n, cap, width)
        exchange(trac_s.at[k], trac_r.at[k], 2 + 2 * k)

    def solid(k, displacement):
        finish(trac_r.at[k], a2a_rs.at[2 + 2 * k])
        got = trac_r[k].reshape(n * cap, width)
        total = load[...] + pick(choose_t[...], got)
        mismatch = product(total, compliance[...]) - displacement
        part = jnp.sum(jnp.sum(mismatch * mismatch, axis=0, keepdims=True), axis=1, keepdims=True)
        return displacement + RELAX * mismatch, part

    sweep(1)
    sweep(2)
    edges = wall_of(0)
    sweep(3)
    for copy in edges:
        copy.wait_recv()
    carried = change(0, [])
    send_traction(0, carried)
    for y in range(SWEEPS):
        force[y] = carried[y]
    sweep(4)
    displacement, part0 = solid(0, init[...])
    wall_s[1] = pick(choose[...], displacement).reshape(n, cap, width)
    exchange(wall_s.at[1], wall_r.at[1], 3)
    disp_out[...] = displacement
    sweep(5)
    last = odd if GHOST % 2 == 1 else even
    bulk = pltpu.make_async_copy(
        last.at[pl.ds(PAD, rows), pl.ds(PAD, depth - PAD)],
        state_out.at[:, pl.ds(PAD, depth - PAD)],
        out_sem.at[0],
    )
    bulk.start()
    edges2 = wall_of(1)
    for copy in edges2:
        copy.wait_recv()
    carried = change(1, [force[y] for y in range(SWEEPS)])
    send_traction(1, carried)
    for y in range(TOTAL):
        last[PAD:end, y, :] = last[PAD:end, y, :] + carried[y][PAD:end, :]
    top = pltpu.make_async_copy(
        last.at[pl.ds(PAD, rows), pl.ds(0, PAD)],
        state_out.at[:, pl.ds(0, PAD)],
        out_sem.at[1],
    )
    top.start()
    displacement, part1 = solid(1, disp_out[...])
    across = iota((1, width), 1)
    row_of_parts = jnp.where(across == 0, part0, jnp.where(across == 1, part1, 0.0))
    norm_s[...] = jnp.broadcast_to(row_of_parts.reshape(1, 1, width), (n, 1, width))
    exchange(norm_s, norm_r, 5)
    disp_out[...] = displacement

    for copy in ghosts + edges + edges2:
        copy.wait_send()
    finish(req_s, a2a_ss.at[0])
    for k in range(COUPLE):
        finish(wall_s.at[k], a2a_ss.at[1 + 2 * k])
        finish(trac_s.at[k], a2a_ss.at[2 + 2 * k])
    bulk.wait()
    top.wait()
    finish(norm_s, a2a_ss.at[5])
    finish(norm_r, a2a_rs.at[5])
    sums = jnp.sum(norm_r[...], axis=0)
    roots = jnp.sqrt(sums + 1e-06)
    for k in range(COUPLE):
        norm_out[k] = jnp.sum(jnp.where(across == k, roots, 0.0))


def per_device(
    n, dom, fluid_source, coef_ids, coef_table, owner_device, owner_slot,
    solid_init, solid_load, compliance,
):
    rows, depth, width = fluid_source.shape
    solid_rows = solid_init.shape[0]
    tall = rows + 2 * PAD
    f32, bf16 = jnp.float32, jnp.bfloat16
    vmem = pl.BlockSpec(memory_space=pltpu.VMEM)
    smem = pl.BlockSpec(memory_space=pltpu.SMEM)
    anywhere = pl.BlockSpec(memory_space=pl.ANY)
    block = (COUPLE, n, PAD, width)
    return tuple(
        pl.pallas_call(
            functools.partial(kernel, n, dom),
            out_shape=(
                jax.ShapeDtypeStruct((rows, depth, width), f32),
                jax.ShapeDtypeStruct((solid_rows, width), f32),
                jax.ShapeDtypeStruct((COUPLE,), f32),
            ),
            in_specs=[anywhere, anywhere, smem, vmem, vmem, vmem, vmem, vmem],
            out_specs=(anywhere, vmem, smem),
            scratch_shapes=[
                pltpu.VMEM((tall, depth, width), f32),
                pltpu.VMEM((tall, depth, width), jnp.int32),
                pltpu.VMEM((tall, depth, width), f32),
                pltpu.VMEM((tall, depth, width), f32),
                pltpu.VMEM((tall, depth, width), f32),
                pltpu.VMEM((TOTAL, tall, width), f32),
                pltpu.VMEM((COUPLE, rows, width), f32),
                pltpu.VMEM((COUPLE, tall, width), f32),
                pltpu.VMEM((SWEEPS, tall, width), f32),
                pltpu.VMEM((n * PAD, rows), bf16),
                pltpu.VMEM((rows, n * PAD), bf16),
                pltpu.VMEM((n * PAD, solid_rows), bf16),
                pltpu.VMEM((solid_rows, n * PAD), bf16),
                pltpu.VMEM((n, 1, width), jnp.int32),
                pltpu.VMEM((n, 1, width), jnp.int32),
                pltpu.VMEM(block, f32),
                pltpu.VMEM(block, f32),
                pltpu.VMEM(block, f32),
                pltpu.VMEM(block, f32),
                pltpu.VMEM((n, 1, width), f32),
                pltpu.VMEM((n, 1, width), f32),
                pltpu.SemaphoreType.DMA((2,)),
                pltpu.SemaphoreType.DMA((2,)),
                pltpu.SemaphoreType.DMA((2, 2)),
                pltpu.SemaphoreType.DMA((2, 2)),
                pltpu.SemaphoreType.DMA((2 + 2 * COUPLE,)),
                pltpu.SemaphoreType.DMA((2 + 2 * COUPLE,)),
                pltpu.SemaphoreType.DMA((COUPLE, 2)),
                pltpu.SemaphoreType.DMA((COUPLE, 2)),
            ],
            compiler_params=pltpu.CompilerParams(
                collective_id=0, has_side_effects=True, vmem_limit_bytes=48 * 2**20
            ),
        )(
            fluid_source, coef_ids, coef_table,
            owner_device.reshape(1, rows), owner_slot.reshape(1, rows),
            solid_init, solid_load, compliance,
        )
    )


def solution(mesh):
    rows = P(("sect", "dom"), None)
    cells = P(("sect", "dom"), None, None)
    n = mesh.shape["sect"] * mesh.shape["dom"]
    return jax.shard_map(
        functools.partial(per_device, n, mesh.shape["dom"]),
        mesh=mesh,
        in_specs=(cells, cells, P(), rows, rows, rows, rows, P()),
        out_specs=(cells, rows, P()),
        check_vma=False,
    )
```

```python
import functools

import jax
import jax.numpy as jnp
from jax import lax
from jax.experimental import pallas as pl
from jax.experimental.pallas import tpu as pltpu
from jax.sharding import PartitionSpec as P

SWEEPS = 3
COUPLE = 2
RELAX = 0.5
TOTAL = SWEEPS * COUPLE
GHOST = TOTAL - 1
PAD = 8
VMEM = 58 * 2**20
MESH = pl.DeviceIdType.MESH


def iota(shape, dim):
    return lax.broadcasted_iota(jnp.int32, shape, dim)


def pieces(x):
    high = x.astype(jnp.bfloat16)
    low = (x - high.astype(jnp.float32)).astype(jnp.bfloat16)
    return high, low


def pick(onehot, x):
    width = x.shape[1]
    both = jnp.concatenate(pieces(x), axis=1)
    out = jnp.dot(onehot, both, preferred_element_type=jnp.float32)
    return out[:, :width] + out[:, width:]


def product(x, y):
    xh, xl = pieces(x)
    yh, yl = pieces(y)
    left = jnp.concatenate([xh, xh, xl], axis=1)
    right = jnp.concatenate([yh, yl, yh], axis=0)
    return jnp.dot(left, right, preferred_element_type=jnp.float32)


def beside(x):
    rows, width = x.shape
    lane = iota(x.shape, 1)
    low = jnp.where(lane == 0, 0.0, pltpu.roll(x, 1, 1))
    high = jnp.where(lane == width - 1, 0.0, pltpu.roll(x, width - 1, 1))
    return low + high


def kernel(
    n, dom, source, ids, table_in, owner_in, slot_in, init_in, load_in, compliance_in,
    state_out, disp_out, norm_out,
    table, owner, slot, init, load, compliance,
    src, idv, inv, even, odd, invp, base, walls, force, trac, disp,
    place, place_t, choose, choose_t,
    req_s, req_r, wall_s, wall_r, trac_s, trac_r, norm_s, norm_r,
    in_sem, out_sem, ghost_ss, ghost_rs, a2a_ss, a2a_rs, edge_ss, edge_rs,
):
    rows, depth, width = source.shape
    end = PAD + rows
    cap = PAD
    sect = n // dom
    my_sect, my_dom = lax.axis_index("sect"), lax.axis_index("dom")
    me = my_sect * dom + my_dom

    def after(sect_at, dom_at):
        over = dom_at + 1 == dom
        dom_next = jnp.where(over, 0, dom_at + 1)
        sect_next = jnp.where(over, sect_at + 1, sect_at)
        return jnp.where(sect_next == sect, 0, sect_next), dom_next

    def ahead(sect_at, dom_at):
        under = dom_at == 0
        dom_next = jnp.where(under, dom - 1, dom_at - 1)
        sect_next = jnp.where(under, sect_at - 1, sect_at)
        return jnp.where(sect_next < 0, sect - 1, sect_next), dom_next

    right = after(my_sect, my_dom)
    left = ahead(my_sect, my_dom)

    def each_peer(act):
        def one(k, at):
            act(*at)
            return after(*at)

        beyond = jnp.where(my_sect + 1 == sect, 0, my_sect + 1)
        at = lax.fori_loop(0, n - dom, one, (beyond, my_dom))
        lax.fori_loop(1, dom, one, after(*at))

    loads = [
        pltpu.make_async_copy(a, b, in_sem.at[i])
        for i, (a, b) in enumerate((
            (owner_in, owner), (slot_in, slot), (table_in, table),
            (ids, idv.at[pl.ds(PAD, rows)]), (source, src.at[pl.ds(PAD, rows)]),
            (init_in, init), (load_in, load), (compliance_in, compliance),
        ))
    ]
    for copy in loads[:2]:
        copy.start()

    barrier = pltpu.get_barrier_semaphore()
    each_peer(lambda *at: pl.semaphore_signal(
        barrier, inc=1, device_id=at, device_id_type=MESH
    ))
    for copy in loads[2:]:
        copy.start()
    for copy in loads[:2]:
        copy.wait()

    owner_row = owner[...]
    slot_row = slot[...]
    hits = (iota((n, rows), 0) == owner_row).astype(jnp.float32)
    before = (iota((rows, rows), 0) < iota((rows, rows), 1)).astype(jnp.bfloat16)
    earlier = jnp.dot(hits.astype(jnp.bfloat16), before, preferred_element_type=jnp.float32)
    rank = jnp.sum(earlier * hits, axis=0, keepdims=True).astype(jnp.int32)
    position = owner_row * cap + rank
    placed = (iota((n * cap, rows), 0) == position).astype(jnp.float32)
    place[...] = placed.astype(jnp.bfloat16)
    place_t[...] = placed.T.astype(jnp.bfloat16)
    wanted = jnp.sum(placed * (slot_row + 1).astype(jnp.float32), axis=1, keepdims=True) - 1.0
    wanted = wanted.reshape(n, cap, 1)
    square = iota((n, cap, width), 2) == iota((n, cap, width), 1)
    req_s[...] = jnp.sum(jnp.where(square, wanted, 0.0), axis=1, keepdims=True).astype(jnp.int32)

    pl.semaphore_wait(barrier, n - 1)

    def exchange(sent, got, phase):
        def one(sect_at, dom_at):
            pltpu.make_async_remote_copy(
                src_ref=sent.at[sect_at * dom + dom_at],
                dst_ref=got.at[me],
                send_sem=a2a_ss.at[phase],
                recv_sem=a2a_rs.at[phase],
                device_id=(sect_at, dom_at),
                device_id_type=MESH,
            ).start()

        each_peer(one)
        got[me] = sent[me]

    def finish(ref, sem):
        part = ref.at[pl.ds(0, n - 1)]
        pltpu.make_async_copy(part, part, sem).wait()

    exchange(req_s, req_r, 0)

    def to_neighbours(from_low, from_high, to_low, to_high, ss, rs):
        copies = [
            pltpu.make_async_remote_copy(
                src_ref=a, dst_ref=b, send_sem=ss(i), recv_sem=rs(i),
                device_id=device, device_id_type=MESH,
            )
            for i, (a, b, device) in enumerate(
                ((from_low, to_high, left), (from_high, to_low, right))
            )
        ]
        for copy in copies:
            copy.start()
        return copies

    ghosts = []
    for number, (whole, held) in enumerate(((source, src), (ids, idv))):
        ghosts += to_neighbours(
            whole.at[pl.ds(0, GHOST)], whole.at[pl.ds(rows - GHOST, GHOST)],
            held.at[pl.ds(PAD - GHOST, GHOST)], held.at[pl.ds(end, GHOST)],
            lambda i: ghost_ss.at[number, i], lambda i: ghost_rs.at[number, i],
        )

    for copy in loads[2:]:
        copy.wait()

    lane = iota((depth, width), 1)
    recip = jnp.zeros((depth, width), jnp.float32)
    for entry in range(table.shape[0]):
        recip = jnp.where(lane == entry, table[entry], recip)
    recip = 1.0 / (6.0 + recip)

    def first(x, scale):
        value = jnp.take_along_axis(recip, idv[x], axis=1, mode="promise_in_bounds")
        if scale is not None:
            value = value * scale
        inv[x] = value
        even[x] = src[x] * value

    def first_block(i, carry):
        for j in range(4):
            first(PAD + 4 * i + j, None)
        return carry

    lax.fori_loop(0, rows // 4, first_block, 0)
    for x in list(range(PAD - GHOST)) + list(range(end + GHOST, end + PAD)):
        inv[x] = jnp.zeros((depth, width), jnp.float32)

    finish(req_r, a2a_rs.at[0])
    slots = jnp.sum(jnp.where(square, req_r[...].astype(jnp.float32), 0.0), axis=2, keepdims=True)
    chosen = (iota((n, cap, init.shape[0]), 2).astype(jnp.float32) == slots).astype(jnp.float32)
    chosen = chosen.reshape(n * cap, init.shape[0])
    choose[...] = chosen.astype(jnp.bfloat16)
    choose_t[...] = chosen.T.astype(jnp.bfloat16)

    wall_s[0] = pick(choose[...], init[...]).reshape(n, cap, width)
    exchange(wall_s.at[0], wall_r.at[0], 1)

    for copy in ghosts:
        copy.wait_recv()
    low_scale = jnp.where(me == 0, 0.0, 1.0)
    high_scale = jnp.where(me == n - 1, 0.0, 1.0)
    for x in range(GHOST):
        first(PAD - GHOST + x, low_scale)
        first(end + x, high_scale)
    for y in range(TOTAL):
        invp[y] = inv[:, y, :]

    row = iota((depth, width), 0)

    def sweep(number):
        old, new = (even, odd) if number % 2 == 1 else (odd, even)
        begin = PAD - (GHOST - number)
        count = rows + 2 * (GHOST - number)

        def planes(x, many):
            held = [old[x - 1 + j] for j in range(many + 2)]
            for j in range(many):
                here = held[j + 1]
                total = src[x + j] + (held[j] + held[j + 2])
                up = jnp.where(row == 0, 0.0, pltpu.roll(here, 1, 0))
                down = jnp.where(row == depth - 1, 0.0, pltpu.roll(here, depth - 1, 0))
                total = total + (up + down) + beside(here)
                new[x + j] = total * inv[x + j]

        def block(i, carry):
            planes(begin + 4 * i, 4)
            return carry

        lax.fori_loop(0, count // 4, block, 0)
        if count % 4:
            planes(begin + count // 4 * 4, count % 4)
        if number % SWEEPS == SWEEPS - 1:
            base[number // SWEEPS] = (
                new[PAD:end, 0, :] - new[PAD:end, 1, :]
            )

    def wall_of(k):
        finish(wall_r.at[k], a2a_rs.at[1 + 2 * k])
        got = wall_r[k].reshape(n * cap, width)
        mine = pick(place_t[...], got)
        walls[k, PAD:end, :] = mine
        held = walls.at[k]
        return mine, to_neighbours(
            held.at[pl.ds(PAD, PAD)], held.at[pl.ds(rows, PAD)],
            held.at[pl.ds(0, PAD)], held.at[pl.ds(end, PAD)],
            lambda i: edge_ss.at[k, i], lambda i: edge_rs.at[k, i],
        )

    def spread(wall, begun, factor):
        found = {}

        def plane(step, y):
            if y >= len(begun) + step:
                return None
            if step == 0:
                return begun[y]
            if (step, y) not in found:
                terms = [wall] if y == 0 else []
                here = plane(step - 1, y)
                if here is not None:
                    tall = here.shape[0]
                    terms.append(pltpu.roll(here, 1, 0) + pltpu.roll(here, tall - 1, 0))
                    terms.append(beside(here))
                if y > 0:
                    terms.append(plane(step - 1, y - 1))
                terms.append(plane(step - 1, y + 1))
                terms = [term for term in terms if term is not None]
                found[step, y] = functools.reduce(jnp.add, terms) * factor(y)
            return found[step, y]

        return plane

    def iterate(k, begun):
        mine, edges = wall_of(k)
        margin = jnp.zeros((PAD, width), jnp.float32)
        own = spread(jnp.concatenate([margin, mine, margin], axis=0), begun, lambda y: invp[y])
        traction = base[k] + (own(SWEEPS, 0) - own(SWEEPS, 1))[PAD:end, :]
        trac[...] = traction
        for copy in edges:
            copy.wait_recv()

        outer = jnp.concatenate(
            [walls[k, :PAD, :], margin, margin, walls[k, end:, :]], axis=0
        )
        other = spread(outer, [], lambda y: jnp.concatenate(
            [invp[y, :2 * PAD, :], invp[y, end - PAD:, :]], axis=0
        ))
        jump = other(SWEEPS, 0) - other(SWEEPS, 1)
        trac[:PAD, :] = trac[:PAD, :] + jump[PAD:2 * PAD, :]
        trac[rows - PAD:, :] = trac[rows - PAD:, :] + jump[2 * PAD:3 * PAD, :]
        trac_s[k] = pick(place[...], trac[...]).reshape(n, cap, width)
        exchange(trac_s.at[k], trac_r.at[k], 2 + 2 * k)
        middle = jnp.zeros((rows - 2 * PAD, width), jnp.float32)
        planes = []
        for y in range(len(begun) + SWEEPS):
            total = own(SWEEPS, y)
            if y < SWEEPS:
                share = other(SWEEPS, y)
                total = total + jnp.concatenate(
                    [share[:2 * PAD, :], middle, share[2 * PAD:, :]], axis=0
                )
            planes.append(total)
        return planes, edges

    def solid(k, displacement):
        finish(trac_r.at[k], a2a_rs.at[2 + 2 * k])
        got = trac_r[k].reshape(n * cap, width)
        total = load[...] + pick(choose_t[...], got)
        mismatch = product(total, compliance[...]) - displacement
        part = jnp.sum(jnp.sum(mismatch * mismatch, axis=0, keepdims=True), axis=1, keepdims=True)
        return displacement + RELAX * mismatch, part

    sweep(1)
    sweep(2)
    planes, edges = iterate(0, [])
    for y in range(SWEEPS):
        force[y] = planes[y]
    sweep(3)
    sweep(4)
    displacement, part0 = solid(0, init[...])
    wall_s[1] = pick(choose[...], displacement).reshape(n, cap, width)
    exchange(wall_s.at[1], wall_r.at[1], 3)
    disp[...] = displacement
    sweep(5)
    last = odd if GHOST % 2 == 1 else even
    bulk = pltpu.make_async_copy(
        last.at[pl.ds(PAD, rows), pl.ds(PAD, depth - PAD)],
        state_out.at[:, pl.ds(PAD, depth - PAD)],
        out_sem.at[0],
    )
    bulk.start()
    planes, edges2 = iterate(1, [force[y] for y in range(SWEEPS)])
    for y in range(TOTAL):
        last[PAD:end, y, :] = last[PAD:end, y, :] + planes[y][PAD:end, :]
    top = pltpu.make_async_copy(
        last.at[pl.ds(PAD, rows), pl.ds(0, PAD)],
        state_out.at[:, pl.ds(0, PAD)],
        out_sem.at[1],
    )
    top.start()
    displacement, part1 = solid(1, disp[...])
    across = iota((1, width), 1)
    row_of_parts = jnp.where(across == 0, part0, jnp.where(across == 1, part1, 0.0))
    norm_s[...] = jnp.broadcast_to(row_of_parts.reshape(1, 1, width), (n, 1, width))
    exchange(norm_s, norm_r, 5)
    disp[...] = displacement
    moved = pltpu.make_async_copy(disp, disp_out, out_sem.at[2])
    moved.start()

    for copy in ghosts + edges + edges2:
        copy.wait_send()
    finish(req_s, a2a_ss.at[0])
    for k in range(COUPLE):
        finish(wall_s.at[k], a2a_ss.at[1 + 2 * k])
        finish(trac_s.at[k], a2a_ss.at[2 + 2 * k])
    bulk.wait()
    top.wait()
    moved.wait()
    finish(norm_s, a2a_ss.at[5])
    finish(norm_r, a2a_rs.at[5])
    norm_out[...] = jnp.sum(norm_r[...], axis=0)


def store_kernel(state, disp, sums, state_out, disp_out, norm_out, held, sem):
    parts = 8
    arrive = pltpu.make_async_copy(sums, held, sem.at[parts + 1])
    arrive.start()
    rows = state.shape[0] // parts
    copies = [pltpu.make_async_copy(disp, disp_out, sem.at[parts])]
    for i in range(parts):
        part = pl.ds(i * rows, rows)
        copies.append(pltpu.make_async_copy(state.at[part], state_out.at[part], sem.at[i]))
    for copy in copies:
        copy.start()
    arrive.wait()
    roots = jnp.sqrt(held[...] + 1e-06)
    across = iota(roots.shape, 1)
    for k in range(COUPLE):
        norm_out[k] = jnp.sum(jnp.where(across == k, roots, 0.0))
    for copy in copies:
        copy.wait()


def per_device(
    n, dom, fluid_source, coef_ids, coef_table, owner_device, owner_slot,
    solid_init, solid_load, compliance,
):
    rows, depth, width = fluid_source.shape
    solid_rows = solid_init.shape[0]
    tall = rows + 2 * PAD
    f32, bf16 = jnp.float32, jnp.bfloat16
    vmem = pl.BlockSpec(memory_space=pltpu.VMEM)
    smem = pl.BlockSpec(memory_space=pltpu.SMEM)
    hbm = pl.BlockSpec(memory_space=pltpu.HBM)
    block = (COUPLE, n, PAD, width)
    state, disp, sums = (
        pl.pallas_call(
            functools.partial(kernel, n, dom),
            out_shape=(
                jax.ShapeDtypeStruct((rows, depth, width), f32),
                jax.ShapeDtypeStruct((solid_rows, width), f32),
                jax.ShapeDtypeStruct((1, width), f32),
            ),
            in_specs=[hbm] * 8,
            out_specs=(hbm, hbm, vmem),
            scratch_shapes=[
                pltpu.SMEM(coef_table.shape, f32),
                pltpu.VMEM((1, rows), jnp.int32),
                pltpu.VMEM((1, rows), jnp.int32),
                pltpu.VMEM((solid_rows, width), f32),
                pltpu.VMEM((solid_rows, width), f32),
                pltpu.VMEM((width, width), f32),
                pltpu.VMEM((tall, depth, width), f32),
                pltpu.VMEM((tall, depth, width), jnp.int32),
                pltpu.VMEM((tall, depth, width), f32),
                pltpu.VMEM((tall, depth, width), f32),
                pltpu.VMEM((tall, depth, width), f32),
                pltpu.VMEM((TOTAL, tall, width), f32),
                pltpu.VMEM((COUPLE, rows, width), f32),
                pltpu.VMEM((COUPLE, tall, width), f32),
                pltpu.VMEM((SWEEPS, tall, width), f32),
                pltpu.VMEM((rows, width), f32),
                pltpu.VMEM((solid_rows, width), f32),
                pltpu.VMEM((n * PAD, rows), bf16),
                pltpu.VMEM((rows, n * PAD), bf16),
                pltpu.VMEM((n * PAD, solid_rows), bf16),
                pltpu.VMEM((solid_rows, n * PAD), bf16),
                pltpu.VMEM((n, 1, width), jnp.int32),
                pltpu.VMEM((n, 1, width), jnp.int32),
                pltpu.VMEM(block, f32),
                pltpu.VMEM(block, f32),
                pltpu.VMEM(block, f32),
                pltpu.VMEM(block, f32),
                pltpu.VMEM((n, 1, width), f32),
                pltpu.VMEM((n, 1, width), f32),
                pltpu.SemaphoreType.DMA((8,)),
                pltpu.SemaphoreType.DMA((3,)),
                pltpu.SemaphoreType.DMA((2, 2)),
                pltpu.SemaphoreType.DMA((2, 2)),
                pltpu.SemaphoreType.DMA((2 + 2 * COUPLE,)),
                pltpu.SemaphoreType.DMA((2 + 2 * COUPLE,)),
                pltpu.SemaphoreType.DMA((COUPLE, 2)),
                pltpu.SemaphoreType.DMA((COUPLE, 2)),
            ],
            compiler_params=pltpu.CompilerParams(
                collective_id=0, has_side_effects=True, vmem_limit_bytes=VMEM
            ),
        )(
            fluid_source, coef_ids, coef_table,
            owner_device.reshape(1, rows), owner_slot.reshape(1, rows),
            solid_init, solid_load, compliance,
        )
    )
    return tuple(
        pl.pallas_call(
            store_kernel,
            out_shape=(
                jax.ShapeDtypeStruct(state.shape, f32),
                jax.ShapeDtypeStruct(disp.shape, f32),
                jax.ShapeDtypeStruct((COUPLE,), f32),
            ),
            in_specs=[hbm] * 3,
            out_specs=(hbm, hbm, smem),
            scratch_shapes=[pltpu.VMEM(sums.shape, f32), pltpu.SemaphoreType.DMA((10,))],
            compiler_params=pltpu.CompilerParams(vmem_limit_bytes=VMEM),
        )(state, disp, sums)
    )


def solution(mesh):
    rows = P(("sect", "dom"), None)
    cells = P(("sect", "dom"), None, None)
    n = mesh.shape["sect"] * mesh.shape["dom"]
    return jax.shard_map(
        functools.partial(per_device, n, mesh.shape["dom"]),
        mesh=mesh,
        in_specs=(cells, cells, P(), rows, rows, rows, rows, P()),
        out_specs=(cells, rows, P()),
        check_vma=False,
    )
```

```python
import functools

import jax
import jax.numpy as jnp
from jax import lax
from jax.experimental import pallas as pl
from jax.experimental.pallas import tpu as pltpu
from jax.sharding import PartitionSpec as P

SWEEPS = 3
COUPLE = 2
RELAX = 0.5
TOTAL = SWEEPS * COUPLE
GHOST = TOTAL - 1
PAD = 8
VMEM = 58 * 2**20
MESH = pl.DeviceIdType.MESH


def iota(shape, dim):
    return lax.broadcasted_iota(jnp.int32, shape, dim)


def pieces(x):
    high = x.astype(jnp.bfloat16)
    low = (x - high.astype(jnp.float32)).astype(jnp.bfloat16)
    return high, low


def pick(onehot, x):
    width = x.shape[1]
    both = jnp.concatenate(pieces(x), axis=1)
    out = jnp.dot(onehot, both, preferred_element_type=jnp.float32)
    return out[:, :width] + out[:, width:]


def product(x, y):
    xh, xl = pieces(x)
    yh, yl = pieces(y)
    left = jnp.concatenate([xh, xh, xl], axis=1)
    right = jnp.concatenate([yh, yl, yh], axis=0)
    return jnp.dot(left, right, preferred_element_type=jnp.float32)


def beside(x):
    rows, width = x.shape
    lane = iota(x.shape, 1)
    low = jnp.where(lane == 0, 0.0, pltpu.roll(x, 1, 1))
    high = jnp.where(lane == width - 1, 0.0, pltpu.roll(x, width - 1, 1))
    return low + high


def kernel(
    n, dom, source, ids, table_in, owner_in, slot_in, init_in, load_in, compliance_in,
    state_out, disp_out, norm_out,
    table, owner, slot, init, load, compliance,
    src, idv, inv, even, odd, invp, base, walls, force, trac, disp,
    place, place_t, choose, choose_t,
    req_s, req_r, wall_s, wall_r, trac_s, trac_r, norm_s, norm_r,
    in_sem, out_sem, ghost_ss, ghost_rs, a2a_ss, a2a_rs, edge_ss, edge_rs,
):
    rows, depth, width = source.shape
    end = PAD + rows
    cap = PAD
    sect = n // dom
    my_sect, my_dom = lax.axis_index("sect"), lax.axis_index("dom")
    me = my_sect * dom + my_dom

    def after(sect_at, dom_at):
        over = dom_at + 1 == dom
        dom_next = jnp.where(over, 0, dom_at + 1)
        sect_next = jnp.where(over, sect_at + 1, sect_at)
        return jnp.where(sect_next == sect, 0, sect_next), dom_next

    def ahead(sect_at, dom_at):
        under = dom_at == 0
        dom_next = jnp.where(under, dom - 1, dom_at - 1)
        sect_next = jnp.where(under, sect_at - 1, sect_at)
        return jnp.where(sect_next < 0, sect - 1, sect_next), dom_next

    right = after(my_sect, my_dom)
    left = ahead(my_sect, my_dom)

    def each_peer(act):
        def one(k, at):
            act(*at)
            return after(*at)

        beyond = jnp.where(my_sect + 1 == sect, 0, my_sect + 1)
        at = lax.fori_loop(0, n - dom, one, (beyond, my_dom))
        lax.fori_loop(1, dom, one, after(*at))

    loads = [
        pltpu.make_async_copy(a, b, in_sem.at[i])
        for i, (a, b) in enumerate((
            (owner_in, owner), (slot_in, slot), (table_in, table),
            (ids, idv.at[pl.ds(PAD, rows)]), (source, src.at[pl.ds(PAD, rows)]),
            (init_in, init), (load_in, load), (compliance_in, compliance),
        ))
    ]
    for copy in loads[:2]:
        copy.start()

    barrier = pltpu.get_barrier_semaphore()
    each_peer(lambda *at: pl.semaphore_signal(
        barrier, inc=1, device_id=at, device_id_type=MESH
    ))
    for copy in loads[2:]:
        copy.start()
    for copy in loads[:2]:
        copy.wait()

    owner_row = owner[...]
    slot_row = slot[...]
    hits = (iota((n, rows), 0) == owner_row).astype(jnp.float32)
    before = (iota((rows, rows), 0) < iota((rows, rows), 1)).astype(jnp.bfloat16)
    earlier = jnp.dot(hits.astype(jnp.bfloat16), before, preferred_element_type=jnp.float32)
    rank = jnp.sum(earlier * hits, axis=0, keepdims=True).astype(jnp.int32)
    position = owner_row * cap + rank
    placed = (iota((n * cap, rows), 0) == position).astype(jnp.float32)
    place[...] = placed.astype(jnp.bfloat16)
    wanted = jnp.sum(placed * (slot_row + 1).astype(jnp.float32), axis=1, keepdims=True) - 1.0
    wanted = wanted.reshape(n, cap, 1)
    square = iota((n, cap, width), 2) == iota((n, cap, width), 1)
    req_s[...] = jnp.sum(jnp.where(square, wanted, 0.0), axis=1, keepdims=True).astype(jnp.int32)

    for copy in loads[2:]:
        copy.wait()

    lane = iota((depth, width), 1)
    recip = jnp.zeros((depth, width), jnp.float32)
    for entry in range(table.shape[0]):
        recip = jnp.where(lane == entry, table[entry], recip)
    recip = 1.0 / (6.0 + recip)

    def first(x, scale):
        value = jnp.take_along_axis(recip, idv[x], axis=1, mode="promise_in_bounds")
        if scale is not None:
            value = value * scale
        inv[x] = value
        even[x] = src[x] * value

    def first_block(i, carry):
        for j in range(4):
            first(PAD + 4 * i + j, None)
        return carry

    lax.fori_loop(0, rows // 4, first_block, 0)
    pl.semaphore_wait(barrier, n - 1)

    def exchange(sent, got, phase):
        def one(sect_at, dom_at):
            pltpu.make_async_remote_copy(
                src_ref=sent.at[sect_at * dom + dom_at],
                dst_ref=got.at[me],
                send_sem=a2a_ss.at[phase],
                recv_sem=a2a_rs.at[phase],
                device_id=(sect_at, dom_at),
                device_id_type=MESH,
            ).start()

        each_peer(one)
        got[me] = sent[me]

    def finish(ref, sem):
        part = ref.at[pl.ds(0, n - 1)]
        pltpu.make_async_copy(part, part, sem).wait()

    exchange(req_s, req_r, 0)
    place_t[...] = placed.T.astype(jnp.bfloat16)

    def to_neighbours(from_low, from_high, to_low, to_high, ss, rs):
        copies = [
            pltpu.make_async_remote_copy(
                src_ref=a, dst_ref=b, send_sem=ss(i), recv_sem=rs(i),
                device_id=device, device_id_type=MESH,
            )
            for i, (a, b, device) in enumerate(
                ((from_low, to_high, left), (from_high, to_low, right))
            )
        ]
        for copy in copies:
            copy.start()
        return copies

    ghosts = []
    for number, (whole, held) in enumerate(((source, src), (ids, idv))):
        ghosts += to_neighbours(
            whole.at[pl.ds(0, GHOST)], whole.at[pl.ds(rows - GHOST, GHOST)],
            held.at[pl.ds(PAD - GHOST, GHOST)], held.at[pl.ds(end, GHOST)],
            lambda i: ghost_ss.at[number, i], lambda i: ghost_rs.at[number, i],
        )

    row = iota((depth, width), 0)

    def sweep(number, begin, stop):
        old, new = (even, odd) if number % 2 == 1 else (odd, even)
        count = stop - begin

        def planes(x, many):
            held = [old[x - 1 + j] for j in range(many + 2)]
            for j in range(many):
                here = held[j + 1]
                total = src[x + j] + (held[j] + held[j + 2])
                up = jnp.where(row == 0, 0.0, pltpu.roll(here, 1, 0))
                down = jnp.where(row == depth - 1, 0.0, pltpu.roll(here, depth - 1, 0))
                total = total + (up + down) + beside(here)
                new[x + j] = total * inv[x + j]

        def block(i, carry):
            planes(begin + 4 * i, 4)
            return carry

        lax.fori_loop(0, count // 4, block, 0)
        if count % 4:
            planes(begin + count // 4 * 4, count % 4)

    def whole(number):
        sweep(number, PAD - (GHOST - number), end + (GHOST - number))

    def tractions(number):
        new = odd if number % 2 == 1 else even
        base[number // SWEEPS] = new[PAD:end, 0, :] - new[PAD:end, 1, :]

    for x in list(range(PAD - GHOST)) + list(range(end + GHOST, end + PAD)):
        inv[x] = jnp.zeros((depth, width), jnp.float32)

    sweep(1, PAD + 1, end - 1)

    finish(req_r, a2a_rs.at[0])
    slots = jnp.sum(jnp.where(square, req_r[...].astype(jnp.float32), 0.0), axis=2, keepdims=True)
    chosen = (iota((n, cap, init.shape[0]), 2).astype(jnp.float32) == slots).astype(jnp.float32)
    chosen = chosen.reshape(n * cap, init.shape[0])
    choose[...] = chosen.astype(jnp.bfloat16)
    wall_s[0] = pick(choose[...], init[...]).reshape(n, cap, width)
    exchange(wall_s.at[0], wall_r.at[0], 1)
    choose_t[...] = chosen.T.astype(jnp.bfloat16)

    for copy in ghosts:
        copy.wait_recv()
    low_scale = jnp.where(me == 0, 0.0, 1.0)
    high_scale = jnp.where(me == n - 1, 0.0, 1.0)
    for x in range(GHOST):
        first(PAD - GHOST + x, low_scale)
        first(end + x, high_scale)
    for y in range(TOTAL):
        invp[y] = inv[:, y, :]

    def wall_of(k):
        finish(wall_r.at[k], a2a_rs.at[1 + 2 * k])
        got = wall_r[k].reshape(n * cap, width)
        mine = pick(place_t[...], got)
        walls[k, PAD:end, :] = mine
        held = walls.at[k]
        return mine, to_neighbours(
            held.at[pl.ds(PAD, PAD)], held.at[pl.ds(rows, PAD)],
            held.at[pl.ds(0, PAD)], held.at[pl.ds(end, PAD)],
            lambda i: edge_ss.at[k, i], lambda i: edge_rs.at[k, i],
        )

    def spread(wall, begun, factor):
        found = {}

        def plane(step, y):
            if y >= len(begun) + step:
                return None
            if step == 0:
                return begun[y]
            if (step, y) not in found:
                terms = [wall] if y == 0 else []
                here = plane(step - 1, y)
                if here is not None:
                    tall = here.shape[0]
                    terms.append(pltpu.roll(here, 1, 0) + pltpu.roll(here, tall - 1, 0))
                    terms.append(beside(here))
                if y > 0:
                    terms.append(plane(step - 1, y - 1))
                terms.append(plane(step - 1, y + 1))
                terms = [term for term in terms if term is not None]
                found[step, y] = functools.reduce(jnp.add, terms) * factor(y)
            return found[step, y]

        return plane

    def iterate(k, begun):
        mine, edges = wall_of(k)
        margin = jnp.zeros((PAD, width), jnp.float32)
        own = spread(jnp.concatenate([margin, mine, margin], axis=0), begun, lambda y: invp[y])
        traction = base[k] + (own(SWEEPS, 0) - own(SWEEPS, 1))[PAD:end, :]
        trac[...] = traction
        for copy in edges:
            copy.wait_recv()

        outer = jnp.concatenate(
            [walls[k, :PAD, :], margin, margin, walls[k, end:, :]], axis=0
        )
        other = spread(outer, [], lambda y: jnp.concatenate(
            [invp[y, :2 * PAD, :], invp[y, end - PAD:, :]], axis=0
        ))
        jump = other(SWEEPS, 0) - other(SWEEPS, 1)
        trac[:PAD, :] = trac[:PAD, :] + jump[PAD:2 * PAD, :]
        trac[rows - PAD:, :] = trac[rows - PAD:, :] + jump[2 * PAD:3 * PAD, :]
        trac_s[k] = pick(place[...], trac[...]).reshape(n, cap, width)
        exchange(trac_s.at[k], trac_r.at[k], 2 + 2 * k)
        middle = jnp.zeros((rows - 2 * PAD, width), jnp.float32)
        planes = []
        for y in range(len(begun) + SWEEPS):
            total = own(SWEEPS, y)
            if y < SWEEPS:
                share = other(SWEEPS, y)
                total = total + jnp.concatenate(
                    [share[:2 * PAD, :], middle, share[2 * PAD:, :]], axis=0
                )
            planes.append(total)
        return planes, edges

    def solid(k, displacement):
        finish(trac_r.at[k], a2a_rs.at[2 + 2 * k])
        got = trac_r[k].reshape(n * cap, width)
        total = load[...] + pick(choose_t[...], got)
        mismatch = product(total, compliance[...]) - displacement
        return displacement + RELAX * mismatch, mismatch

    def squares(mismatch):
        return jnp.sum(jnp.sum(mismatch * mismatch, axis=0, keepdims=True), axis=1, keepdims=True)

    sweep(1, PAD - GHOST + 1, PAD + 1)
    sweep(1, end - 1, end + GHOST - 1)
    whole(2)
    tractions(2)
    planes, edges = iterate(0, [])
    for y in range(SWEEPS):
        force[y] = planes[y]
    whole(3)
    sweep(4, PAD - 1, PAD + rows // 2)
    displacement, mismatch = solid(0, init[...])
    wall_s[1] = pick(choose[...], displacement).reshape(n, cap, width)
    exchange(wall_s.at[1], wall_r.at[1], 3)
    disp[...] = displacement
    part0 = squares(mismatch)
    sweep(4, PAD + rows // 2, end + 1)
    whole(5)
    tractions(5)
    last = odd if GHOST % 2 == 1 else even
    bulk = pltpu.make_async_copy(
        last.at[pl.ds(PAD, rows), pl.ds(PAD, depth - PAD)],
        state_out.at[:, pl.ds(PAD, depth - PAD)],
        out_sem.at[0],
    )
    bulk.start()
    planes, edges2 = iterate(1, [force[y] for y in range(SWEEPS)])
    for y in range(TOTAL):
        last[PAD:end, y, :] = last[PAD:end, y, :] + planes[y][PAD:end, :]
    top = pltpu.make_async_copy(
        last.at[pl.ds(PAD, rows), pl.ds(0, PAD)],
        state_out.at[:, pl.ds(0, PAD)],
        out_sem.at[1],
    )
    top.start()
    displacement, mismatch = solid(1, disp[...])
    part1 = squares(mismatch)
    across = iota((1, width), 1)
    row_of_parts = jnp.where(across == 0, part0, jnp.where(across == 1, part1, 0.0))
    norm_s[...] = jnp.broadcast_to(row_of_parts.reshape(1, 1, width), (n, 1, width))
    exchange(norm_s, norm_r, 5)
    disp[...] = displacement
    moved = pltpu.make_async_copy(disp, disp_out, out_sem.at[2])
    moved.start()

    for copy in ghosts + edges + edges2:
        copy.wait_send()
    finish(req_s, a2a_ss.at[0])
    for k in range(COUPLE):
        finish(wall_s.at[k], a2a_ss.at[1 + 2 * k])
        finish(trac_s.at[k], a2a_ss.at[2 + 2 * k])
    bulk.wait()
    top.wait()
    moved.wait()
    finish(norm_s, a2a_ss.at[5])
    finish(norm_r, a2a_rs.at[5])
    norm_out[...] = jnp.sum(norm_r[...], axis=0)


def store_kernel(state, disp, sums, state_out, disp_out, norm_out, held, moved, added, get, put):
    parts = get.shape[0] - 2
    rows = state.shape[0] // parts
    blocks = [(sums, added, None), (disp, moved, disp_out)]
    for i in range(parts):
        part = pl.ds(i * rows, rows)
        blocks.append((state.at[part], held.at[part], state_out.at[part]))
    arrivals = [
        pltpu.make_async_copy(here, kept, get.at[i]) for i, (here, kept, _) in enumerate(blocks)
    ]
    for copy in arrivals:
        copy.start()
    leaves = []
    for i, (_, kept, there) in enumerate(blocks):
        arrivals[i].wait()
        if there is not None:
            leaves.append(pltpu.make_async_copy(kept, there, put.at[i]))
            leaves[-1].start()
    roots = jnp.sqrt(added[...] + 1e-06)
    across = iota(roots.shape, 1)
    for k in range(COUPLE):
        norm_out[k] = jnp.sum(jnp.where(across == k, roots, 0.0))
    for copy in leaves:
        copy.wait()


def per_device(
    n, dom, fluid_source, coef_ids, coef_table, owner_device, owner_slot,
    solid_init, solid_load, compliance,
):
    rows, depth, width = fluid_source.shape
    solid_rows = solid_init.shape[0]
    tall = rows + 2 * PAD
    f32, bf16 = jnp.float32, jnp.bfloat16
    vmem = pl.BlockSpec(memory_space=pltpu.VMEM)
    smem = pl.BlockSpec(memory_space=pltpu.SMEM)
    hbm = pl.BlockSpec(memory_space=pltpu.HBM)
    block = (COUPLE, n, PAD, width)
    state, disp, sums = (
        pl.pallas_call(
            functools.partial(kernel, n, dom),
            out_shape=(
                jax.ShapeDtypeStruct((rows, depth, width), f32),
                jax.ShapeDtypeStruct((solid_rows, width), f32),
                jax.ShapeDtypeStruct((1, width), f32),
            ),
            in_specs=[hbm] * 8,
            out_specs=(hbm, hbm, vmem),
            scratch_shapes=[
                pltpu.SMEM(coef_table.shape, f32),
                pltpu.VMEM((1, rows), jnp.int32),
                pltpu.VMEM((1, rows), jnp.int32),
                pltpu.VMEM((solid_rows, width), f32),
                pltpu.VMEM((solid_rows, width), f32),
                pltpu.VMEM((width, width), f32),
                pltpu.VMEM((tall, depth, width), f32),
                pltpu.VMEM((tall, depth, width), jnp.int32),
                pltpu.VMEM((tall, depth, width), f32),
                pltpu.VMEM((tall, depth, width), f32),
                pltpu.VMEM((tall, depth, width), f32),
                pltpu.VMEM((TOTAL, tall, width), f32),
                pltpu.VMEM((COUPLE, rows, width), f32),
                pltpu.VMEM((COUPLE, tall, width), f32),
                pltpu.VMEM((SWEEPS, tall, width), f32),
                pltpu.VMEM((rows, width), f32),
                pltpu.VMEM((solid_rows, width), f32),
                pltpu.VMEM((n * PAD, rows), bf16),
                pltpu.VMEM((rows, n * PAD), bf16),
                pltpu.VMEM((n * PAD, solid_rows), bf16),
                pltpu.VMEM((solid_rows, n * PAD), bf16),
                pltpu.VMEM((n, 1, width), jnp.int32),
                pltpu.VMEM((n, 1, width), jnp.int32),
                pltpu.VMEM(block, f32),
                pltpu.VMEM(block, f32),
                pltpu.VMEM(block, f32),
                pltpu.VMEM(block, f32),
                pltpu.VMEM((n, 1, width), f32),
                pltpu.VMEM((n, 1, width), f32),
                pltpu.SemaphoreType.DMA((8,)),
                pltpu.SemaphoreType.DMA((3,)),
                pltpu.SemaphoreType.DMA((2, 2)),
                pltpu.SemaphoreType.DMA((2, 2)),
                pltpu.SemaphoreType.DMA((2 + 2 * COUPLE,)),
                pltpu.SemaphoreType.DMA((2 + 2 * COUPLE,)),
                pltpu.SemaphoreType.DMA((COUPLE, 2)),
                pltpu.SemaphoreType.DMA((COUPLE, 2)),
            ],
            compiler_params=pltpu.CompilerParams(
                collective_id=0, has_side_effects=True, vmem_limit_bytes=VMEM
            ),
        )(
            fluid_source, coef_ids, coef_table,
            owner_device.reshape(1, rows), owner_slot.reshape(1, rows),
            solid_init, solid_load, compliance,
        )
    )
    return tuple(
        pl.pallas_call(
            store_kernel,
            out_shape=(
                jax.ShapeDtypeStruct(state.shape, f32),
                jax.ShapeDtypeStruct(disp.shape, f32),
                jax.ShapeDtypeStruct((COUPLE,), f32),
            ),
            in_specs=[hbm] * 3,
            out_specs=(hbm, hbm, smem),
            scratch_shapes=[
                pltpu.VMEM(state.shape, f32),
                pltpu.VMEM(disp.shape, f32),
                pltpu.VMEM(sums.shape, f32),
                pltpu.SemaphoreType.DMA((10,)),
                pltpu.SemaphoreType.DMA((10,)),
            ],
            compiler_params=pltpu.CompilerParams(vmem_limit_bytes=VMEM),
        )(state, disp, sums)
    )


def solution(mesh):
    rows = P(("sect", "dom"), None)
    cells = P(("sect", "dom"), None, None)
    n = mesh.shape["sect"] * mesh.shape["dom"]
    return jax.shard_map(
        functools.partial(per_device, n, mesh.shape["dom"]),
        mesh=mesh,
        in_specs=(cells, cells, P(), rows, rows, rows, rows, P()),
        out_specs=(cells, rows, P()),
        check_vma=False,
    )
```

```python
import functools

import jax
import jax.numpy as jnp
from jax import lax
from jax.experimental import pallas as pl
from jax.experimental.pallas import tpu as pltpu
from jax.sharding import PartitionSpec as P

SWEEPS = 3
COUPLE = 2
RELAX = 0.5
TOTAL = SWEEPS * COUPLE
GHOST = TOTAL - 1
PAD = 8
VMEM = 58 * 2**20
MESH = pl.DeviceIdType.MESH


def iota(shape, dim):
    return lax.broadcasted_iota(jnp.int32, shape, dim)


def pieces(x):
    high = x.astype(jnp.bfloat16)
    low = (x - high.astype(jnp.float32)).astype(jnp.bfloat16)
    return high, low


def pick(onehot, x):
    width = x.shape[1]
    both = jnp.concatenate(pieces(x), axis=1)
    out = jnp.dot(onehot, both, preferred_element_type=jnp.float32)
    return out[:, :width] + out[:, width:]


def product(x, y):
    xh, xl = pieces(x)
    yh, yl = pieces(y)
    left = jnp.concatenate([xh, xh, xl], axis=1)
    right = jnp.concatenate([yh, yl, yh], axis=0)
    return jnp.dot(left, right, preferred_element_type=jnp.float32)


def beside(x):
    rows, width = x.shape
    lane = iota(x.shape, 1)
    low = jnp.where(lane == 0, 0.0, pltpu.roll(x, 1, 1))
    high = jnp.where(lane == width - 1, 0.0, pltpu.roll(x, width - 1, 1))
    return low + high


def kernel(
    n, dom, source, ids, table_in, owner_in, slot_in, init_in, load_in, compliance_in,
    state_out, disp_out, norm_out,
    table, owner, slot, init, load, compliance,
    src, idv, inv, even, odd, invp, base, walls, force, trac, disp,
    place, place_t, choose, choose_t,
    req_s, req_r, wall_s, wall_r, trac_s, trac_r, norm_s, norm_r,
    in_sem, out_sem, ghost_ss, ghost_rs, a2a_ss, a2a_rs, edge_ss, edge_rs,
):
    rows, depth, width = source.shape
    end = PAD + rows
    cap = PAD
    sect = n // dom
    my_sect, my_dom = lax.axis_index("sect"), lax.axis_index("dom")
    me = my_sect * dom + my_dom

    def after(sect_at, dom_at):
        over = dom_at + 1 == dom
        dom_next = jnp.where(over, 0, dom_at + 1)
        sect_next = jnp.where(over, sect_at + 1, sect_at)
        return jnp.where(sect_next == sect, 0, sect_next), dom_next

    def ahead(sect_at, dom_at):
        under = dom_at == 0
        dom_next = jnp.where(under, dom - 1, dom_at - 1)
        sect_next = jnp.where(under, sect_at - 1, sect_at)
        return jnp.where(sect_next < 0, sect - 1, sect_next), dom_next

    right = after(my_sect, my_dom)
    left = ahead(my_sect, my_dom)

    def wrapped(value, count):
        return jnp.where(value >= count, value - count, value)

    dom_at = [wrapped(my_dom + step, dom) for step in range(dom)]

    def each_peer(act):
        def one(step, carry):
            sect_at = wrapped(my_sect + step, sect)
            for at in dom_at:
                act(sect_at, at)
            return carry

        lax.fori_loop(1, sect, one, 0)
        for at in dom_at[1:]:
            act(my_sect, at)

    loads = [
        pltpu.make_async_copy(a, b, in_sem.at[i])
        for i, (a, b) in enumerate((
            (owner_in, owner), (slot_in, slot), (table_in, table),
            (ids, idv.at[pl.ds(PAD, rows)]), (source, src.at[pl.ds(PAD, rows)]),
            (init_in, init), (load_in, load), (compliance_in, compliance),
        ))
    ]
    for copy in loads[:2]:
        copy.start()

    barrier = pltpu.get_barrier_semaphore()
    each_peer(lambda *at: pl.semaphore_signal(
        barrier, inc=1, device_id=at, device_id_type=MESH
    ))
    for copy in loads[2:]:
        copy.start()
    for copy in loads[:2]:
        copy.wait()

    owner_row = owner[...]
    slot_row = slot[...]
    hits = (iota((n, rows), 0) == owner_row).astype(jnp.float32)
    before = (iota((rows, rows), 0) < iota((rows, rows), 1)).astype(jnp.bfloat16)
    earlier = jnp.dot(hits.astype(jnp.bfloat16), before, preferred_element_type=jnp.float32)
    rank = jnp.sum(earlier * hits, axis=0, keepdims=True).astype(jnp.int32)
    position = owner_row * cap + rank
    placed = (iota((n * cap, rows), 0) == position).astype(jnp.float32)
    place[...] = placed.astype(jnp.bfloat16)
    wanted = jnp.sum(placed * (slot_row + 1).astype(jnp.float32), axis=1, keepdims=True) - 1.0
    wanted = wanted.reshape(n, cap, 1)
    square = iota((n, cap, width), 2) == iota((n, cap, width), 1)
    req_s[...] = jnp.sum(jnp.where(square, wanted, 0.0), axis=1, keepdims=True).astype(jnp.int32)

    for copy in loads[2:]:
        copy.wait()

    lane = iota((depth, width), 1)
    recip = jnp.zeros((depth, width), jnp.float32)
    for entry in range(table.shape[0]):
        recip = jnp.where(lane == entry, table[entry], recip)
    recip = 1.0 / (6.0 + recip)

    def first(x, scale):
        value = jnp.take_along_axis(recip, idv[x], axis=1, mode="promise_in_bounds")
        if scale is not None:
            value = value * scale
        inv[x] = value
        even[x] = src[x] * value

    def first_block(i, carry):
        for j in range(4):
            first(PAD + 4 * i + j, None)
        return carry

    lax.fori_loop(0, rows // 4, first_block, 0)
    pl.semaphore_wait(barrier, n - 1)

    def exchange(sent, got, phase):
        def one(sect_at, dom_at):
            pltpu.make_async_remote_copy(
                src_ref=sent.at[sect_at * dom + dom_at],
                dst_ref=got.at[me],
                send_sem=a2a_ss.at[phase],
                recv_sem=a2a_rs.at[phase],
                device_id=(sect_at, dom_at),
                device_id_type=MESH,
            ).start()

        each_peer(one)
        got[me] = sent[me]

    def finish(ref, sem):
        part = ref.at[pl.ds(0, n - 1)]
        pltpu.make_async_copy(part, part, sem).wait()

    exchange(req_s, req_r, 0)
    place_t[...] = placed.T.astype(jnp.bfloat16)

    def to_neighbours(from_low, from_high, to_low, to_high, ss, rs):
        copies = [
            pltpu.make_async_remote_copy(
                src_ref=a, dst_ref=b, send_sem=ss(i), recv_sem=rs(i),
                device_id=device, device_id_type=MESH,
            )
            for i, (a, b, device) in enumerate(
                ((from_low, to_high, left), (from_high, to_low, right))
            )
        ]
        for copy in copies:
            copy.start()
        return copies

    ghosts = []
    for number, (whole, held) in enumerate(((source, src), (ids, idv))):
        ghosts += to_neighbours(
            whole.at[pl.ds(0, GHOST)], whole.at[pl.ds(rows - GHOST, GHOST)],
            held.at[pl.ds(PAD - GHOST, GHOST)], held.at[pl.ds(end, GHOST)],
            lambda i: ghost_ss.at[number, i], lambda i: ghost_rs.at[number, i],
        )

    row = iota((depth, width), 0)

    def sweep(number, begin, stop):
        old, new = (even, odd) if number % 2 == 1 else (odd, even)
        count = stop - begin

        def planes(x, many):
            held = [old[x - 1 + j] for j in range(many + 2)]
            for j in range(many):
                here = held[j + 1]
                total = src[x + j] + (held[j] + held[j + 2])
                up = jnp.where(row == 0, 0.0, pltpu.roll(here, 1, 0))
                down = jnp.where(row == depth - 1, 0.0, pltpu.roll(here, depth - 1, 0))
                total = total + (up + down) + beside(here)
                new[x + j] = total * inv[x + j]

        def block(i, carry):
            planes(begin + 4 * i, 4)
            return carry

        lax.fori_loop(0, count // 4, block, 0)
        if count % 4:
            planes(begin + count // 4 * 4, count % 4)

    def whole(number):
        sweep(number, PAD - (GHOST - number), end + (GHOST - number))

    def tractions(number):
        new = odd if number % 2 == 1 else even
        base[number // SWEEPS] = new[PAD:end, 0, :] - new[PAD:end, 1, :]

    for x in list(range(PAD - GHOST)) + list(range(end + GHOST, end + PAD)):
        inv[x] = jnp.zeros((depth, width), jnp.float32)

    sweep(1, PAD + 1, end - 1)

    finish(req_r, a2a_rs.at[0])
    slots = jnp.sum(jnp.where(square, req_r[...].astype(jnp.float32), 0.0), axis=2, keepdims=True)
    chosen = (iota((n, cap, init.shape[0]), 2).astype(jnp.float32) == slots).astype(jnp.float32)
    chosen = chosen.reshape(n * cap, init.shape[0])
    choose[...] = chosen.astype(jnp.bfloat16)
    wall_s[0] = pick(choose[...], init[...]).reshape(n, cap, width)
    exchange(wall_s.at[0], wall_r.at[0], 1)
    choose_t[...] = chosen.T.astype(jnp.bfloat16)

    for copy in ghosts:
        copy.wait_recv()
    low_scale = jnp.where(me == 0, 0.0, 1.0)
    high_scale = jnp.where(me == n - 1, 0.0, 1.0)
    for x in range(GHOST):
        first(PAD - GHOST + x, low_scale)
        first(end + x, high_scale)
    for y in range(TOTAL):
        invp[y] = inv[:, y, :]

    def wall_of(k):
        finish(wall_r.at[k], a2a_rs.at[1 + 2 * k])
        got = wall_r[k].reshape(n * cap, width)
        mine = pick(place_t[...], got)
        walls[k, PAD:end, :] = mine
        held = walls.at[k]
        return mine, to_neighbours(
            held.at[pl.ds(PAD, PAD)], held.at[pl.ds(rows, PAD)],
            held.at[pl.ds(0, PAD)], held.at[pl.ds(end, PAD)],
            lambda i: edge_ss.at[k, i], lambda i: edge_rs.at[k, i],
        )

    def spread(wall, begun, factor):
        found = {}

        def plane(step, y):
            if y >= len(begun) + step:
                return None
            if step == 0:
                return begun[y]
            if (step, y) not in found:
                terms = [wall] if y == 0 else []
                here = plane(step - 1, y)
                if here is not None:
                    tall = here.shape[0]
                    terms.append(pltpu.roll(here, 1, 0) + pltpu.roll(here, tall - 1, 0))
                    terms.append(beside(here))
                if y > 0:
                    terms.append(plane(step - 1, y - 1))
                terms.append(plane(step - 1, y + 1))
                terms = [term for term in terms if term is not None]
                found[step, y] = functools.reduce(jnp.add, terms) * factor(y)
            return found[step, y]

        return plane

    def iterate(k, begun):
        mine, edges = wall_of(k)
        margin = jnp.zeros((PAD, width), jnp.float32)
        own = spread(jnp.concatenate([margin, mine, margin], axis=0), begun, lambda y: invp[y])
        traction = base[k] + (own(SWEEPS, 0) - own(SWEEPS, 1))[PAD:end, :]
        trac[...] = traction
        for copy in edges:
            copy.wait_recv()

        outer = jnp.concatenate(
            [walls[k, :PAD, :], margin, margin, walls[k, end:, :]], axis=0
        )
        other = spread(outer, [], lambda y: jnp.concatenate(
            [invp[y, :2 * PAD, :], invp[y, end - PAD:, :]], axis=0
        ))
        jump = other(SWEEPS, 0) - other(SWEEPS, 1)
        trac[:PAD, :] = trac[:PAD, :] + jump[PAD:2 * PAD, :]
        trac[rows - PAD:, :] = trac[rows - PAD:, :] + jump[2 * PAD:3 * PAD, :]
        trac_s[k] = pick(place[...], trac[...]).reshape(n, cap, width)
        exchange(trac_s.at[k], trac_r.at[k], 2 + 2 * k)
        middle = jnp.zeros((rows - 2 * PAD, width), jnp.float32)
        planes = []
        for y in range(len(begun) + SWEEPS):
            total = own(SWEEPS, y)
            if y < SWEEPS:
                share = other(SWEEPS, y)
                total = total + jnp.concatenate(
                    [share[:2 * PAD, :], middle, share[2 * PAD:, :]], axis=0
                )
            planes.append(total)
        return planes, edges

    def solid(k, displacement):
        finish(trac_r.at[k], a2a_rs.at[2 + 2 * k])
        got = trac_r[k].reshape(n * cap, width)
        total = load[...] + pick(choose_t[...], got)
        mismatch = product(total, compliance[...]) - displacement
        return displacement + RELAX * mismatch, mismatch

    def squares(mismatch):
        return jnp.sum(jnp.sum(mismatch * mismatch, axis=0, keepdims=True), axis=1, keepdims=True)

    sweep(1, PAD - GHOST + 1, PAD + 1)
    sweep(1, end - 1, end + GHOST - 1)
    whole(2)
    tractions(2)
    planes, edges = iterate(0, [])
    for y in range(SWEEPS):
        force[y] = planes[y]
    whole(3)
    sweep(4, PAD - 1, PAD + rows // 2)
    displacement, mismatch = solid(0, init[...])
    wall_s[1] = pick(choose[...], displacement).reshape(n, cap, width)
    exchange(wall_s.at[1], wall_r.at[1], 3)
    disp[...] = displacement
    part0 = squares(mismatch)
    sweep(4, PAD + rows // 2, end + 1)
    whole(5)
    tractions(5)
    last = odd if GHOST % 2 == 1 else even
    bulk = pltpu.make_async_copy(
        last.at[pl.ds(PAD, rows), pl.ds(PAD, depth - PAD)],
        state_out.at[:, pl.ds(PAD, depth - PAD)],
        out_sem.at[0],
    )
    bulk.start()
    planes, edges2 = iterate(1, [force[y] for y in range(SWEEPS)])
    for y in range(TOTAL):
        last[PAD:end, y, :] = last[PAD:end, y, :] + planes[y][PAD:end, :]
    top = pltpu.make_async_copy(
        last.at[pl.ds(PAD, rows), pl.ds(0, PAD)],
        state_out.at[:, pl.ds(0, PAD)],
        out_sem.at[1],
    )
    top.start()
    displacement, mismatch = solid(1, disp[...])
    part1 = squares(mismatch)
    across = iota((1, width), 1)
    row_of_parts = jnp.where(across == 0, part0, jnp.where(across == 1, part1, 0.0))
    norm_s[...] = jnp.broadcast_to(row_of_parts.reshape(1, 1, width), (n, 1, width))
    exchange(norm_s, norm_r, 5)
    disp[...] = displacement
    moved = pltpu.make_async_copy(disp, disp_out, out_sem.at[2])
    moved.start()

    for copy in ghosts + edges + edges2:
        copy.wait_send()
    finish(req_s, a2a_ss.at[0])
    for k in range(COUPLE):
        finish(wall_s.at[k], a2a_ss.at[1 + 2 * k])
        finish(trac_s.at[k], a2a_ss.at[2 + 2 * k])
    bulk.wait()
    top.wait()
    moved.wait()
    finish(norm_s, a2a_ss.at[5])
    finish(norm_r, a2a_rs.at[5])
    norm_out[...] = jnp.sum(norm_r[...], axis=0)


def store_kernel(state, disp, sums, state_out, disp_out, norm_out, held, moved, added, get, put):
    parts = get.shape[0] - 2
    rows = state.shape[0] // parts
    blocks = [(sums, added, None), (disp, moved, disp_out)]
    for i in range(parts):
        part = pl.ds(i * rows, rows)
        blocks.append((state.at[part], held.at[part], state_out.at[part]))
    arrivals = [
        pltpu.make_async_copy(here, kept, get.at[i]) for i, (here, kept, _) in enumerate(blocks)
    ]
    for copy in arrivals:
        copy.start()
    leaves = []
    for i, (_, kept, there) in enumerate(blocks):
        arrivals[i].wait()
        if there is not None:
            leaves.append(pltpu.make_async_copy(kept, there, put.at[i]))
            leaves[-1].start()
    roots = jnp.sqrt(added[...] + 1e-06)
    across = iota(roots.shape, 1)
    for k in range(COUPLE):
        norm_out[k] = jnp.sum(jnp.where(across == k, roots, 0.0))
    for copy in leaves:
        copy.wait()


def per_device(
    n, dom, fluid_source, coef_ids, coef_table, owner_device, owner_slot,
    solid_init, solid_load, compliance,
):
    rows, depth, width = fluid_source.shape
    solid_rows = solid_init.shape[0]
    tall = rows + 2 * PAD
    f32, bf16 = jnp.float32, jnp.bfloat16
    vmem = pl.BlockSpec(memory_space=pltpu.VMEM)
    smem = pl.BlockSpec(memory_space=pltpu.SMEM)
    hbm = pl.BlockSpec(memory_space=pltpu.HBM)
    block = (COUPLE, n, PAD, width)
    state, disp, sums = (
        pl.pallas_call(
            functools.partial(kernel, n, dom),
            out_shape=(
                jax.ShapeDtypeStruct((rows, depth, width), f32),
                jax.ShapeDtypeStruct((solid_rows, width), f32),
                jax.ShapeDtypeStruct((1, width), f32),
            ),
            in_specs=[hbm] * 8,
            out_specs=(hbm, hbm, vmem),
            scratch_shapes=[
                pltpu.SMEM(coef_table.shape, f32),
                pltpu.VMEM((1, rows), jnp.int32),
                pltpu.VMEM((1, rows), jnp.int32),
                pltpu.VMEM((solid_rows, width), f32),
                pltpu.VMEM((solid_rows, width), f32),
                pltpu.VMEM((width, width), f32),
                pltpu.VMEM((tall, depth, width), f32),
                pltpu.VMEM((tall, depth, width), jnp.int32),
                pltpu.VMEM((tall, depth, width), f32),
                pltpu.VMEM((tall, depth, width), f32),
                pltpu.VMEM((tall, depth, width), f32),
                pltpu.VMEM((TOTAL, tall, width), f32),
                pltpu.VMEM((COUPLE, rows, width), f32),
                pltpu.VMEM((COUPLE, tall, width), f32),
                pltpu.VMEM((SWEEPS, tall, width), f32),
                pltpu.VMEM((rows, width), f32),
                pltpu.VMEM((solid_rows, width), f32),
                pltpu.VMEM((n * PAD, rows), bf16),
                pltpu.VMEM((rows, n * PAD), bf16),
                pltpu.VMEM((n * PAD, solid_rows), bf16),
                pltpu.VMEM((solid_rows, n * PAD), bf16),
                pltpu.VMEM((n, 1, width), jnp.int32),
                pltpu.VMEM((n, 1, width), jnp.int32),
                pltpu.VMEM(block, f32),
                pltpu.VMEM(block, f32),
                pltpu.VMEM(block, f32),
                pltpu.VMEM(block, f32),
                pltpu.VMEM((n, 1, width), f32),
                pltpu.VMEM((n, 1, width), f32),
                pltpu.SemaphoreType.DMA((8,)),
                pltpu.SemaphoreType.DMA((3,)),
                pltpu.SemaphoreType.DMA((2, 2)),
                pltpu.SemaphoreType.DMA((2, 2)),
                pltpu.SemaphoreType.DMA((2 + 2 * COUPLE,)),
                pltpu.SemaphoreType.DMA((2 + 2 * COUPLE,)),
                pltpu.SemaphoreType.DMA((COUPLE, 2)),
                pltpu.SemaphoreType.DMA((COUPLE, 2)),
            ],
            compiler_params=pltpu.CompilerParams(
                collective_id=0, has_side_effects=True, vmem_limit_bytes=VMEM
            ),
        )(
            fluid_source, coef_ids, coef_table,
            owner_device.reshape(1, rows), owner_slot.reshape(1, rows),
            solid_init, solid_load, compliance,
        )
    )
    return tuple(
        pl.pallas_call(
            store_kernel,
            out_shape=(
                jax.ShapeDtypeStruct(state.shape, f32),
                jax.ShapeDtypeStruct(disp.shape, f32),
                jax.ShapeDtypeStruct((COUPLE,), f32),
            ),
            in_specs=[hbm] * 3,
            out_specs=(hbm, hbm, smem),
            scratch_shapes=[
                pltpu.VMEM(state.shape, f32),
                pltpu.VMEM(disp.shape, f32),
                pltpu.VMEM(sums.shape, f32),
                pltpu.SemaphoreType.DMA((10,)),
                pltpu.SemaphoreType.DMA((10,)),
            ],
            compiler_params=pltpu.CompilerParams(vmem_limit_bytes=VMEM),
        )(state, disp, sums)
    )


def solution(mesh):
    rows = P(("sect", "dom"), None)
    cells = P(("sect", "dom"), None, None)
    n = mesh.shape["sect"] * mesh.shape["dom"]
    return jax.shard_map(
        functools.partial(per_device, n, mesh.shape["dom"]),
        mesh=mesh,
        in_specs=(cells, cells, P(), rows, rows, rows, rows, P()),
        out_specs=(cells, rows, P()),
        check_vma=False,
    )
```

```python
import functools

import jax
import jax.numpy as jnp
from jax import lax
from jax.experimental import pallas as pl
from jax.experimental.pallas import tpu as pltpu
from jax.sharding import PartitionSpec as P

SWEEPS = 3
COUPLE = 2
RELAX = 0.5
TOTAL = SWEEPS * COUPLE
GHOST = TOTAL - 1
PAD = 8
STEP = 8
VMEM = 58 * 2**20
MESH = pl.DeviceIdType.MESH


def iota(shape, dim):
    return lax.broadcasted_iota(jnp.int32, shape, dim)


def pieces(x):
    high = x.astype(jnp.bfloat16)
    low = (x - high.astype(jnp.float32)).astype(jnp.bfloat16)
    return high, low


def pick(onehot, x):
    width = x.shape[1]
    both = jnp.concatenate(pieces(x), axis=1)
    out = jnp.dot(onehot, both, preferred_element_type=jnp.float32)
    return out[:, :width] + out[:, width:]


def product(x, y):
    xh, xl = pieces(x)
    yh, yl = pieces(y)
    left = jnp.concatenate([xh, xh, xl], axis=1)
    right = jnp.concatenate([yh, yl, yh], axis=0)
    return jnp.dot(left, right, preferred_element_type=jnp.float32)


def beside(x):
    rows, width = x.shape
    lane = iota(x.shape, 1)
    low = jnp.where(lane == 0, 0.0, pltpu.roll(x, 1, 1))
    high = jnp.where(lane == width - 1, 0.0, pltpu.roll(x, width - 1, 1))
    return low + high


def kernel(
    n, dom, source, ids, table_in, owner_in, slot_in, init_in, load_in, compliance_in,
    state_out, disp_out, norm_out,
    table, owner, slot, init, load, compliance,
    src, idv, inv, even, odd, invp, base, walls, force, trac, disp,
    place, place_t, choose, choose_t,
    req_s, req_r, wall_s, wall_r, trac_s, trac_r, norm_s, norm_r,
    in_sem, out_sem, ghost_ss, ghost_rs, a2a_ss, a2a_rs, edge_ss, edge_rs,
):
    rows, depth, width = source.shape
    end = PAD + rows
    cap = PAD
    sect = n // dom
    my_sect, my_dom = lax.axis_index("sect"), lax.axis_index("dom")
    me = my_sect * dom + my_dom

    def after(sect_at, dom_at):
        over = dom_at + 1 == dom
        dom_next = jnp.where(over, 0, dom_at + 1)
        sect_next = jnp.where(over, sect_at + 1, sect_at)
        return jnp.where(sect_next == sect, 0, sect_next), dom_next

    def ahead(sect_at, dom_at):
        under = dom_at == 0
        dom_next = jnp.where(under, dom - 1, dom_at - 1)
        sect_next = jnp.where(under, sect_at - 1, sect_at)
        return jnp.where(sect_next < 0, sect - 1, sect_next), dom_next

    right = after(my_sect, my_dom)
    left = ahead(my_sect, my_dom)

    def wrapped(value, count):
        return jnp.where(value >= count, value - count, value)

    dom_at = [wrapped(my_dom + step, dom) for step in range(dom)]

    def each_peer(act):
        def one(step, carry):
            sect_at = wrapped(my_sect + step, sect)
            for at in dom_at:
                act(sect_at, at)
            return carry

        lax.fori_loop(1, sect, one, 0)
        for at in dom_at[1:]:
            act(my_sect, at)

    loads = [
        pltpu.make_async_copy(a, b, in_sem.at[i])
        for i, (a, b) in enumerate((
            (owner_in, owner), (slot_in, slot), (table_in, table),
            (ids, idv.at[pl.ds(PAD, rows)]), (source, src.at[pl.ds(PAD, rows)]),
            (init_in, init), (load_in, load), (compliance_in, compliance),
        ))
    ]
    for copy in loads[:2]:
        copy.start()

    barrier = pltpu.get_barrier_semaphore()
    each_peer(lambda *at: pl.semaphore_signal(
        barrier, inc=1, device_id=at, device_id_type=MESH
    ))
    for copy in loads[2:]:
        copy.start()
    for copy in loads[:2]:
        copy.wait()

    owner_row = owner[...]
    slot_row = slot[...]
    hits = (iota((n, rows), 0) == owner_row).astype(jnp.float32)
    before = (iota((rows, rows), 0) < iota((rows, rows), 1)).astype(jnp.bfloat16)
    earlier = jnp.dot(hits.astype(jnp.bfloat16), before, preferred_element_type=jnp.float32)
    rank = jnp.sum(earlier * hits, axis=0, keepdims=True).astype(jnp.int32)
    position = owner_row * cap + rank
    placed = (iota((n * cap, rows), 0) == position).astype(jnp.float32)
    place[...] = placed.astype(jnp.bfloat16)
    wanted = jnp.sum(placed * (slot_row + 1).astype(jnp.float32), axis=1, keepdims=True) - 1.0
    wanted = wanted.reshape(n, cap, 1)
    square = iota((n, cap, width), 2) == iota((n, cap, width), 1)
    req_s[...] = jnp.sum(jnp.where(square, wanted, 0.0), axis=1, keepdims=True).astype(jnp.int32)

    for copy in loads[2:]:
        copy.wait()

    lane = iota((depth, width), 1)
    recip = jnp.zeros((depth, width), jnp.float32)
    for entry in range(table.shape[0]):
        recip = jnp.where(lane == entry, table[entry], recip)
    recip = 1.0 / (6.0 + recip)

    def first(x, scale):
        value = jnp.take_along_axis(recip, idv[x], axis=1, mode="promise_in_bounds")
        if scale is not None:
            value = value * scale
        inv[x] = value
        even[x] = src[x] * value

    def first_block(i, carry):
        for j in range(STEP):
            first(PAD + STEP * i + j, None)
        return carry

    lax.fori_loop(0, rows // STEP, first_block, 0)
    pl.semaphore_wait(barrier, n - 1)

    def exchange(sent, got, phase):
        def one(sect_at, dom_at):
            pltpu.make_async_remote_copy(
                src_ref=sent.at[sect_at * dom + dom_at],
                dst_ref=got.at[me],
                send_sem=a2a_ss.at[phase],
                recv_sem=a2a_rs.at[phase],
                device_id=(sect_at, dom_at),
                device_id_type=MESH,
            ).start()

        each_peer(one)
        got[me] = sent[me]

    def finish(ref, sem):
        part = ref.at[pl.ds(0, n - 1)]
        pltpu.make_async_copy(part, part, sem).wait()

    exchange(req_s, req_r, 0)
    place_t[...] = placed.T.astype(jnp.bfloat16)

    def to_neighbours(from_low, from_high, to_low, to_high, ss, rs):
        copies = [
            pltpu.make_async_remote_copy(
                src_ref=a, dst_ref=b, send_sem=ss(i), recv_sem=rs(i),
                device_id=device, device_id_type=MESH,
            )
            for i, (a, b, device) in enumerate(
                ((from_low, to_high, left), (from_high, to_low, right))
            )
        ]
        for copy in copies:
            copy.start()
        return copies

    ghosts = []
    for number, (whole, held) in enumerate(((source, src), (ids, idv))):
        ghosts += to_neighbours(
            whole.at[pl.ds(0, GHOST)], whole.at[pl.ds(rows - GHOST, GHOST)],
            held.at[pl.ds(PAD - GHOST, GHOST)], held.at[pl.ds(end, GHOST)],
            lambda i: ghost_ss.at[number, i], lambda i: ghost_rs.at[number, i],
        )

    low_row = iota((8, width), 0) == 0
    high_row = iota((8, width), 0) == 7

    def sweep(number, begin, stop):
        old, new = (even, odd) if number % 2 == 1 else (odd, even)
        count = stop - begin

        flat = old.reshape(old.shape[0] * depth, width)

        def planes(x, many):
            held = [old[x - 1 + j] for j in range(many + 2)]
            for j in range(many):
                here = held[j + 1]
                at = (x + j) * depth
                up = flat[pl.ds(at - 1, depth), :]
                down = flat[pl.ds(at + 1, depth), :]
                up = jnp.concatenate([jnp.where(low_row, 0.0, up[:8]), up[8:]], axis=0)
                down = jnp.concatenate([down[:-8], jnp.where(high_row, 0.0, down[-8:])], axis=0)
                total = src[x + j] + (held[j] + held[j + 2])
                total = total + (up + down) + beside(here)
                new[x + j] = total * inv[x + j]

        def block(i, carry):
            planes(begin + STEP * i, STEP)
            return carry

        lax.fori_loop(0, count // STEP, block, 0)
        if count % STEP:
            planes(begin + count // STEP * STEP, count % STEP)

    def whole(number):
        sweep(number, PAD - (GHOST - number), end + (GHOST - number))

    def tractions(number):
        new = odd if number % 2 == 1 else even
        base[number // SWEEPS] = new[PAD:end, 0, :] - new[PAD:end, 1, :]

    for x in list(range(PAD - GHOST)) + list(range(end + GHOST, end + PAD)):
        inv[x] = jnp.zeros((depth, width), jnp.float32)

    sweep(1, PAD + 1, end - 1)

    finish(req_r, a2a_rs.at[0])
    slots = jnp.sum(jnp.where(square, req_r[...].astype(jnp.float32), 0.0), axis=2, keepdims=True)
    chosen = (iota((n, cap, init.shape[0]), 2).astype(jnp.float32) == slots).astype(jnp.float32)
    chosen = chosen.reshape(n * cap, init.shape[0])
    choose[...] = chosen.astype(jnp.bfloat16)
    wall_s[0] = pick(choose[...], init[...]).reshape(n, cap, width)
    exchange(wall_s.at[0], wall_r.at[0], 1)
    choose_t[...] = chosen.T.astype(jnp.bfloat16)

    for copy in ghosts:
        copy.wait_recv()
    low_scale = jnp.where(me == 0, 0.0, 1.0)
    high_scale = jnp.where(me == n - 1, 0.0, 1.0)
    for x in range(GHOST):
        first(PAD - GHOST + x, low_scale)
        first(end + x, high_scale)
    for y in range(TOTAL):
        invp[y] = inv[:, y, :]

    def wall_of(k):
        finish(wall_r.at[k], a2a_rs.at[1 + 2 * k])
        got = wall_r[k].reshape(n * cap, width)
        mine = pick(place_t[...], got)
        walls[k, PAD:end, :] = mine
        held = walls.at[k]
        return mine, to_neighbours(
            held.at[pl.ds(PAD, PAD)], held.at[pl.ds(rows, PAD)],
            held.at[pl.ds(0, PAD)], held.at[pl.ds(end, PAD)],
            lambda i: edge_ss.at[k, i], lambda i: edge_rs.at[k, i],
        )

    def spread(wall, begun, factor):
        found = {}

        def plane(step, y):
            if y >= len(begun) + step:
                return None
            if step == 0:
                return begun[y]
            if (step, y) not in found:
                terms = [wall] if y == 0 else []
                here = plane(step - 1, y)
                if here is not None:
                    tall = here.shape[0]
                    terms.append(pltpu.roll(here, 1, 0) + pltpu.roll(here, tall - 1, 0))
                    terms.append(beside(here))
                if y > 0:
                    terms.append(plane(step - 1, y - 1))
                terms.append(plane(step - 1, y + 1))
                terms = [term for term in terms if term is not None]
                found[step, y] = functools.reduce(jnp.add, terms) * factor(y)
            return found[step, y]

        return plane

    def iterate(k, begun):
        mine, edges = wall_of(k)
        margin = jnp.zeros((PAD, width), jnp.float32)
        own = spread(jnp.concatenate([margin, mine, margin], axis=0), begun, lambda y: invp[y])
        traction = base[k] + (own(SWEEPS, 0) - own(SWEEPS, 1))[PAD:end, :]
        trac[...] = traction
        for copy in edges:
            copy.wait_recv()

        outer = jnp.concatenate(
            [walls[k, :PAD, :], margin, margin, walls[k, end:, :]], axis=0
        )
        other = spread(outer, [], lambda y: jnp.concatenate(
            [invp[y, :2 * PAD, :], invp[y, end - PAD:, :]], axis=0
        ))
        jump = other(SWEEPS, 0) - other(SWEEPS, 1)
        trac[:PAD, :] = trac[:PAD, :] + jump[PAD:2 * PAD, :]
        trac[rows - PAD:, :] = trac[rows - PAD:, :] + jump[2 * PAD:3 * PAD, :]
        trac_s[k] = pick(place[...], trac[...]).reshape(n, cap, width)
        exchange(trac_s.at[k], trac_r.at[k], 2 + 2 * k)
        middle = jnp.zeros((rows - 2 * PAD, width), jnp.float32)
        planes = []
        for y in range(len(begun) + SWEEPS):
            total = own(SWEEPS, y)
            if y < SWEEPS:
                share = other(SWEEPS, y)
                total = total + jnp.concatenate(
                    [share[:2 * PAD, :], middle, share[2 * PAD:, :]], axis=0
                )
            planes.append(total)
        return planes, edges

    def solid(k, displacement):
        finish(trac_r.at[k], a2a_rs.at[2 + 2 * k])
        got = trac_r[k].reshape(n * cap, width)
        total = load[...] + pick(choose_t[...], got)
        mismatch = product(total, compliance[...]) - displacement
        return displacement + RELAX * mismatch, mismatch

    def squares(mismatch):
        return jnp.sum(jnp.sum(mismatch * mismatch, axis=0, keepdims=True), axis=1, keepdims=True)

    sweep(1, PAD - GHOST + 1, PAD + 1)
    sweep(1, end - 1, end + GHOST - 1)
    whole(2)
    tractions(2)
    planes, edges = iterate(0, [])
    for y in range(SWEEPS):
        force[y] = planes[y]
    whole(3)
    sweep(4, PAD - 1, PAD + rows // 2)
    displacement, mismatch = solid(0, init[...])
    wall_s[1] = pick(choose[...], displacement).reshape(n, cap, width)
    exchange(wall_s.at[1], wall_r.at[1], 3)
    disp[...] = displacement
    part0 = squares(mismatch)
    sweep(4, PAD + rows // 2, end + 1)
    whole(5)
    tractions(5)
    last = odd if GHOST % 2 == 1 else even
    bulk = pltpu.make_async_copy(
        last.at[pl.ds(PAD, rows), pl.ds(PAD, depth - PAD)],
        state_out.at[:, pl.ds(PAD, depth - PAD)],
        out_sem.at[0],
    )
    bulk.start()
    planes, edges2 = iterate(1, [force[y] for y in range(SWEEPS)])
    for y in range(TOTAL):
        last[PAD:end, y, :] = last[PAD:end, y, :] + planes[y][PAD:end, :]
    top = pltpu.make_async_copy(
        last.at[pl.ds(PAD, rows), pl.ds(0, PAD)],
        state_out.at[:, pl.ds(0, PAD)],
        out_sem.at[1],
    )
    top.start()
    displacement, mismatch = solid(1, disp[...])
    part1 = squares(mismatch)
    across = iota((1, width), 1)
    row_of_parts = jnp.where(across == 0, part0, jnp.where(across == 1, part1, 0.0))
    norm_s[...] = jnp.broadcast_to(row_of_parts.reshape(1, 1, width), (n, 1, width))
    exchange(norm_s, norm_r, 5)
    disp[...] = displacement
    moved = pltpu.make_async_copy(disp, disp_out, out_sem.at[2])
    moved.start()

    for copy in ghosts + edges + edges2:
        copy.wait_send()
    finish(req_s, a2a_ss.at[0])
    for k in range(COUPLE):
        finish(wall_s.at[k], a2a_ss.at[1 + 2 * k])
        finish(trac_s.at[k], a2a_ss.at[2 + 2 * k])
    bulk.wait()
    top.wait()
    moved.wait()
    finish(norm_s, a2a_ss.at[5])
    finish(norm_r, a2a_rs.at[5])
    norm_out[...] = jnp.sum(norm_r[...], axis=0)


def store_kernel(state, disp, sums, state_out, disp_out, norm_out, held, moved, added, get, put):
    parts = get.shape[0] - 2
    rows = state.shape[0] // parts
    blocks = [(sums, added, None), (disp, moved, disp_out)]
    for i in range(parts):
        part = pl.ds(i * rows, rows)
        blocks.append((state.at[part], held.at[part], state_out.at[part]))
    arrivals = [
        pltpu.make_async_copy(here, kept, get.at[i]) for i, (here, kept, _) in enumerate(blocks)
    ]
    for copy in arrivals:
        copy.start()
    leaves = []
    for i, (_, kept, there) in enumerate(blocks):
        arrivals[i].wait()
        if there is not None:
            leaves.append(pltpu.make_async_copy(kept, there, put.at[i]))
            leaves[-1].start()
    roots = jnp.sqrt(added[...] + 1e-06)
    across = iota(roots.shape, 1)
    for k in range(COUPLE):
        norm_out[k] = jnp.sum(jnp.where(across == k, roots, 0.0))
    for copy in leaves:
        copy.wait()


def per_device(
    n, dom, fluid_source, coef_ids, coef_table, owner_device, owner_slot,
    solid_init, solid_load, compliance,
):
    rows, depth, width = fluid_source.shape
    solid_rows = solid_init.shape[0]
    tall = rows + 2 * PAD
    f32, bf16 = jnp.float32, jnp.bfloat16
    vmem = pl.BlockSpec(memory_space=pltpu.VMEM)
    smem = pl.BlockSpec(memory_space=pltpu.SMEM)
    hbm = pl.BlockSpec(memory_space=pltpu.HBM)
    block = (COUPLE, n, PAD, width)
    state, disp, sums = (
        pl.pallas_call(
            functools.partial(kernel, n, dom),
            out_shape=(
                jax.ShapeDtypeStruct((rows, depth, width), f32),
                jax.ShapeDtypeStruct((solid_rows, width), f32),
                jax.ShapeDtypeStruct((1, width), f32),
            ),
            in_specs=[hbm] * 8,
            out_specs=(hbm, hbm, vmem),
            scratch_shapes=[
                pltpu.SMEM(coef_table.shape, f32),
                pltpu.VMEM((1, rows), jnp.int32),
                pltpu.VMEM((1, rows), jnp.int32),
                pltpu.VMEM((solid_rows, width), f32),
                pltpu.VMEM((solid_rows, width), f32),
                pltpu.VMEM((width, width), f32),
                pltpu.VMEM((tall, depth, width), f32),
                pltpu.VMEM((tall, depth, width), jnp.int32),
                pltpu.VMEM((tall, depth, width), f32),
                pltpu.VMEM((tall, depth, width), f32),
                pltpu.VMEM((tall, depth, width), f32),
                pltpu.VMEM((TOTAL, tall, width), f32),
                pltpu.VMEM((COUPLE, rows, width), f32),
                pltpu.VMEM((COUPLE, tall, width), f32),
                pltpu.VMEM((SWEEPS, tall, width), f32),
                pltpu.VMEM((rows, width), f32),
                pltpu.VMEM((solid_rows, width), f32),
                pltpu.VMEM((n * PAD, rows), bf16),
                pltpu.VMEM((rows, n * PAD), bf16),
                pltpu.VMEM((n * PAD, solid_rows), bf16),
                pltpu.VMEM((solid_rows, n * PAD), bf16),
                pltpu.VMEM((n, 1, width), jnp.int32),
                pltpu.VMEM((n, 1, width), jnp.int32),
                pltpu.VMEM(block, f32),
                pltpu.VMEM(block, f32),
                pltpu.VMEM(block, f32),
                pltpu.VMEM(block, f32),
                pltpu.VMEM((n, 1, width), f32),
                pltpu.VMEM((n, 1, width), f32),
                pltpu.SemaphoreType.DMA((8,)),
                pltpu.SemaphoreType.DMA((3,)),
                pltpu.SemaphoreType.DMA((2, 2)),
                pltpu.SemaphoreType.DMA((2, 2)),
                pltpu.SemaphoreType.DMA((2 + 2 * COUPLE,)),
                pltpu.SemaphoreType.DMA((2 + 2 * COUPLE,)),
                pltpu.SemaphoreType.DMA((COUPLE, 2)),
                pltpu.SemaphoreType.DMA((COUPLE, 2)),
            ],
            compiler_params=pltpu.CompilerParams(
                collective_id=0, has_side_effects=True, vmem_limit_bytes=VMEM
            ),
        )(
            fluid_source, coef_ids, coef_table,
            owner_device.reshape(1, rows), owner_slot.reshape(1, rows),
            solid_init, solid_load, compliance,
        )
    )
    return tuple(
        pl.pallas_call(
            store_kernel,
            out_shape=(
                jax.ShapeDtypeStruct(state.shape, f32),
                jax.ShapeDtypeStruct(disp.shape, f32),
                jax.ShapeDtypeStruct((COUPLE,), f32),
            ),
            in_specs=[hbm] * 3,
            out_specs=(hbm, hbm, smem),
            scratch_shapes=[
                pltpu.VMEM(state.shape, f32),
                pltpu.VMEM(disp.shape, f32),
                pltpu.VMEM(sums.shape, f32),
                pltpu.SemaphoreType.DMA((10,)),
                pltpu.SemaphoreType.DMA((10,)),
            ],
            compiler_params=pltpu.CompilerParams(vmem_limit_bytes=VMEM),
        )(state, disp, sums)
    )


def solution(mesh):
    rows = P(("sect", "dom"), None)
    cells = P(("sect", "dom"), None, None)
    n = mesh.shape["sect"] * mesh.shape["dom"]
    return jax.shard_map(
        functools.partial(per_device, n, mesh.shape["dom"]),
        mesh=mesh,
        in_specs=(cells, cells, P(), rows, rows, rows, rows, P()),
        out_specs=(cells, rows, P()),
        check_vma=False,
    )
```

```python
import functools

import jax
import jax.numpy as jnp
from jax import lax
from jax.experimental import pallas as pl
from jax.experimental.pallas import tpu as pltpu
from jax.sharding import PartitionSpec as P

SWEEPS = 3
COUPLE = 2
RELAX = 0.5
TOTAL = SWEEPS * COUPLE
GHOST = TOTAL - 1
PAD = 8
STEP = 16
VMEM = 58 * 2**20
MESH = pl.DeviceIdType.MESH


def iota(shape, dim):
    return lax.broadcasted_iota(jnp.int32, shape, dim)


def pieces(x):
    high = x.astype(jnp.bfloat16)
    low = (x - high.astype(jnp.float32)).astype(jnp.bfloat16)
    return high, low


def pick(onehot, x):
    width = x.shape[1]
    both = jnp.concatenate(pieces(x), axis=1)
    out = jnp.dot(onehot, both, preferred_element_type=jnp.float32)
    return out[:, :width] + out[:, width:]


def product(x, y):
    xh, xl = pieces(x)
    yh, yl = pieces(y)
    left = jnp.concatenate([xh, xh, xl], axis=1)
    right = jnp.concatenate([yh, yl, yh], axis=0)
    return jnp.dot(left, right, preferred_element_type=jnp.float32)


def beside(x):
    rows, width = x.shape
    lane = iota(x.shape, 1)
    low = jnp.where(lane == 0, 0.0, pltpu.roll(x, 1, 1))
    high = jnp.where(lane == width - 1, 0.0, pltpu.roll(x, width - 1, 1))
    return low + high


def kernel(
    n, dom, source, ids, table_in, owner_in, slot_in, init_in, load_in, compliance_in,
    state_out, disp_out, norm_out,
    table, owner, slot, init, load, compliance,
    src, idv, inv, even, odd, invp, base, walls, force, trac, disp,
    place, place_t, choose, choose_t,
    req_s, req_r, wall_s, wall_r, trac_s, trac_r, norm_s, norm_r,
    in_sem, out_sem, ghost_ss, ghost_rs, a2a_ss, a2a_rs, edge_ss, edge_rs,
):
    rows, depth, width = source.shape
    end = PAD + rows
    cap = PAD
    sect = n // dom
    my_sect, my_dom = lax.axis_index("sect"), lax.axis_index("dom")
    me = my_sect * dom + my_dom

    def after(sect_at, dom_at):
        over = dom_at + 1 == dom
        dom_next = jnp.where(over, 0, dom_at + 1)
        sect_next = jnp.where(over, sect_at + 1, sect_at)
        return jnp.where(sect_next == sect, 0, sect_next), dom_next

    def ahead(sect_at, dom_at):
        under = dom_at == 0
        dom_next = jnp.where(under, dom - 1, dom_at - 1)
        sect_next = jnp.where(under, sect_at - 1, sect_at)
        return jnp.where(sect_next < 0, sect - 1, sect_next), dom_next

    right = after(my_sect, my_dom)
    left = ahead(my_sect, my_dom)

    def wrapped(value, count):
        return jnp.where(value >= count, value - count, value)

    dom_at = [wrapped(my_dom + step, dom) for step in range(dom)]

    def each_peer(act):
        def one(step, carry):
            sect_at = wrapped(my_sect + step, sect)
            for at in dom_at:
                act(sect_at, at)
            return carry

        lax.fori_loop(1, sect, one, 0)
        for at in dom_at[1:]:
            act(my_sect, at)

    loads = [
        pltpu.make_async_copy(a, b, in_sem.at[i])
        for i, (a, b) in enumerate((
            (owner_in, owner), (slot_in, slot), (table_in, table),
            (ids, idv.at[pl.ds(PAD, rows)]), (source, src.at[pl.ds(PAD, rows)]),
            (init_in, init), (load_in, load), (compliance_in, compliance),
        ))
    ]
    for copy in loads[:2]:
        copy.start()

    barrier = pltpu.get_barrier_semaphore()
    each_peer(lambda *at: pl.semaphore_signal(
        barrier, inc=1, device_id=at, device_id_type=MESH
    ))
    for copy in loads[2:]:
        copy.start()
    for copy in loads[:2]:
        copy.wait()

    owner_row = owner[...]
    slot_row = slot[...]
    hits = (iota((n, rows), 0) == owner_row).astype(jnp.float32)
    before = (iota((rows, rows), 0) < iota((rows, rows), 1)).astype(jnp.bfloat16)
    earlier = jnp.dot(hits.astype(jnp.bfloat16), before, preferred_element_type=jnp.float32)
    rank = jnp.sum(earlier * hits, axis=0, keepdims=True).astype(jnp.int32)
    position = owner_row * cap + rank
    placed = (iota((n * cap, rows), 0) == position).astype(jnp.float32)
    place[...] = placed.astype(jnp.bfloat16)
    wanted = jnp.sum(placed * (slot_row + 1).astype(jnp.float32), axis=1, keepdims=True) - 1.0
    wanted = wanted.reshape(n, cap, 1)
    square = iota((n, cap, width), 2) == iota((n, cap, width), 1)
    req_s[...] = jnp.sum(jnp.where(square, wanted, 0.0), axis=1, keepdims=True).astype(jnp.int32)

    for copy in loads[2:]:
        copy.wait()

    lane = iota((depth, width), 1)
    recip = jnp.zeros((depth, width), jnp.float32)
    for entry in range(table.shape[0]):
        recip = jnp.where(lane == entry, table[entry], recip)
    recip = 1.0 / (6.0 + recip)

    def first(x, scale):
        value = jnp.take_along_axis(recip, idv[x], axis=1, mode="promise_in_bounds")
        if scale is not None:
            value = value * scale
        inv[x] = value
        even[x] = src[x] * value

    def first_block(i, carry):
        for j in range(PAD):
            first(PAD + PAD * i + j, None)
        return carry

    lax.fori_loop(0, rows // PAD, first_block, 0)
    pl.semaphore_wait(barrier, n - 1)

    def exchange(sent, got, phase):
        def one(sect_at, dom_at):
            pltpu.make_async_remote_copy(
                src_ref=sent.at[sect_at * dom + dom_at],
                dst_ref=got.at[me],
                send_sem=a2a_ss.at[phase],
                recv_sem=a2a_rs.at[phase],
                device_id=(sect_at, dom_at),
                device_id_type=MESH,
            ).start()

        each_peer(one)
        got[me] = sent[me]

    def finish(ref, sem):
        part = ref.at[pl.ds(0, n - 1)]
        pltpu.make_async_copy(part, part, sem).wait()

    exchange(req_s, req_r, 0)
    place_t[...] = placed.T.astype(jnp.bfloat16)

    def to_neighbours(from_low, from_high, to_low, to_high, ss, rs):
        copies = [
            pltpu.make_async_remote_copy(
                src_ref=a, dst_ref=b, send_sem=ss(i), recv_sem=rs(i),
                device_id=device, device_id_type=MESH,
            )
            for i, (a, b, device) in enumerate(
                ((from_low, to_high, left), (from_high, to_low, right))
            )
        ]
        for copy in copies:
            copy.start()
        return copies

    ghosts = []
    for number, (whole, held) in enumerate(((source, src), (ids, idv))):
        ghosts += to_neighbours(
            whole.at[pl.ds(0, GHOST)], whole.at[pl.ds(rows - GHOST, GHOST)],
            held.at[pl.ds(PAD - GHOST, GHOST)], held.at[pl.ds(end, GHOST)],
            lambda i: ghost_ss.at[number, i], lambda i: ghost_rs.at[number, i],
        )

    def column(ref, begin, count, y):
        flat = ref.reshape(ref.shape[0] * depth, width)
        return flat, pl.ds(begin * depth + y, count, stride=depth)

    def take(ref, begin, count, y):
        flat, where = column(ref, begin, count, y)
        return flat[where, :]

    low_row = iota((8, width), 0) == 0
    high_row = iota((8, width), 0) == 7

    def sweep(number, begin, stop):
        old, new = (even, odd) if number % 2 == 1 else (odd, even)
        count = stop - begin

        flat = old.reshape(old.shape[0] * depth, width)

        def planes(x, many):
            held = [old[x - 1 + j] for j in range(many + 2)]
            for j in range(many):
                here = held[j + 1]
                at = (x + j) * depth
                up = flat[pl.ds(at - 1, depth), :]
                down = flat[pl.ds(at + 1, depth), :]
                up = jnp.concatenate([jnp.where(low_row, 0.0, up[:8]), up[8:]], axis=0)
                down = jnp.concatenate([down[:-8], jnp.where(high_row, 0.0, down[-8:])], axis=0)
                total = src[x + j] + (held[j] + held[j + 2])
                total = total + (up + down) + beside(here)
                new[x + j] = total * inv[x + j]

        blocks = -(-count // STEP)
        step = -(-count // blocks)

        def block(i, carry):
            planes(jnp.where(i == blocks - 1, stop - step, begin + step * i), step)
            return carry

        if blocks == 1:
            planes(begin, count)
        else:
            lax.fori_loop(0, blocks, block, 0)

    def whole(number):
        sweep(number, PAD - (GHOST - number), end + (GHOST - number))

    def tractions(number):
        new = odd if number % 2 == 1 else even
        base[number // SWEEPS] = take(new, PAD, rows, 0) - take(new, PAD, rows, 1)

    for x in list(range(PAD - GHOST)) + list(range(end + GHOST, end + PAD)):
        inv[x] = jnp.zeros((depth, width), jnp.float32)

    sweep(1, PAD + 1, end - 1)

    finish(req_r, a2a_rs.at[0])
    slots = jnp.sum(jnp.where(square, req_r[...].astype(jnp.float32), 0.0), axis=2, keepdims=True)
    chosen = (iota((n, cap, init.shape[0]), 2).astype(jnp.float32) == slots).astype(jnp.float32)
    chosen = chosen.reshape(n * cap, init.shape[0])
    choose[...] = chosen.astype(jnp.bfloat16)
    wall_s[0] = pick(choose[...], init[...]).reshape(n, cap, width)
    exchange(wall_s.at[0], wall_r.at[0], 1)
    choose_t[...] = chosen.T.astype(jnp.bfloat16)

    for copy in ghosts:
        copy.wait_recv()
    low_scale = jnp.where(me == 0, 0.0, 1.0)
    high_scale = jnp.where(me == n - 1, 0.0, 1.0)
    for x in range(GHOST):
        first(PAD - GHOST + x, low_scale)
        first(end + x, high_scale)
    for y in range(TOTAL):
        invp[y] = take(inv, 0, rows + 2 * PAD, y)

    def wall_of(k):
        finish(wall_r.at[k], a2a_rs.at[1 + 2 * k])
        got = wall_r[k].reshape(n * cap, width)
        mine = pick(place_t[...], got)
        walls[k, PAD:end, :] = mine
        held = walls.at[k]
        return mine, to_neighbours(
            held.at[pl.ds(PAD, PAD)], held.at[pl.ds(rows, PAD)],
            held.at[pl.ds(0, PAD)], held.at[pl.ds(end, PAD)],
            lambda i: edge_ss.at[k, i], lambda i: edge_rs.at[k, i],
        )

    def spread(wall, begun, factor):
        found = {}

        def plane(step, y):
            if y >= len(begun) + step:
                return None
            if step == 0:
                return begun[y]
            if (step, y) not in found:
                terms = [wall] if y == 0 else []
                here = plane(step - 1, y)
                if here is not None:
                    tall = here.shape[0]
                    terms.append(pltpu.roll(here, 1, 0) + pltpu.roll(here, tall - 1, 0))
                    terms.append(beside(here))
                if y > 0:
                    terms.append(plane(step - 1, y - 1))
                terms.append(plane(step - 1, y + 1))
                terms = [term for term in terms if term is not None]
                found[step, y] = functools.reduce(jnp.add, terms) * factor(y)
            return found[step, y]

        return plane

    def iterate(k, begun):
        mine, edges = wall_of(k)
        margin = jnp.zeros((PAD, width), jnp.float32)
        own = spread(jnp.concatenate([margin, mine, margin], axis=0), begun, lambda y: invp[y])
        traction = base[k] + (own(SWEEPS, 0) - own(SWEEPS, 1))[PAD:end, :]
        trac[...] = traction
        for copy in edges:
            copy.wait_recv()

        outer = jnp.concatenate(
            [walls[k, :PAD, :], margin, margin, walls[k, end:, :]], axis=0
        )
        other = spread(outer, [], lambda y: jnp.concatenate(
            [invp[y, :2 * PAD, :], invp[y, end - PAD:, :]], axis=0
        ))
        jump = other(SWEEPS, 0) - other(SWEEPS, 1)
        trac[:PAD, :] = trac[:PAD, :] + jump[PAD:2 * PAD, :]
        trac[rows - PAD:, :] = trac[rows - PAD:, :] + jump[2 * PAD:3 * PAD, :]
        trac_s[k] = pick(place[...], trac[...]).reshape(n, cap, width)
        exchange(trac_s.at[k], trac_r.at[k], 2 + 2 * k)
        middle = jnp.zeros((rows - 2 * PAD, width), jnp.float32)
        planes = []
        for y in range(len(begun) + SWEEPS):
            total = own(SWEEPS, y)
            if y < SWEEPS:
                share = other(SWEEPS, y)
                total = total + jnp.concatenate(
                    [share[:2 * PAD, :], middle, share[2 * PAD:, :]], axis=0
                )
            planes.append(total)
        return planes, edges

    def solid(k, displacement):
        finish(trac_r.at[k], a2a_rs.at[2 + 2 * k])
        got = trac_r[k].reshape(n * cap, width)
        total = load[...] + pick(choose_t[...], got)
        mismatch = product(total, compliance[...]) - displacement
        return displacement + RELAX * mismatch, mismatch

    def squares(mismatch):
        return jnp.sum(jnp.sum(mismatch * mismatch, axis=0, keepdims=True), axis=1, keepdims=True)

    sweep(1, PAD - GHOST + 1, PAD + 1)
    sweep(1, end - 1, end + GHOST - 1)
    whole(2)
    tractions(2)
    planes, edges = iterate(0, [])
    for y in range(SWEEPS):
        force[y] = planes[y]
    whole(3)
    sweep(4, PAD - 1, PAD + rows // 2)
    displacement, mismatch = solid(0, init[...])
    wall_s[1] = pick(choose[...], displacement).reshape(n, cap, width)
    exchange(wall_s.at[1], wall_r.at[1], 3)
    disp[...] = displacement
    part0 = squares(mismatch)
    sweep(4, PAD + rows // 2, end + 1)
    whole(5)
    tractions(5)
    last = odd if GHOST % 2 == 1 else even
    bulk = pltpu.make_async_copy(
        last.at[pl.ds(PAD, rows), pl.ds(PAD, depth - PAD)],
        state_out.at[:, pl.ds(PAD, depth - PAD)],
        out_sem.at[0],
    )
    bulk.start()
    planes, edges2 = iterate(1, [force[y] for y in range(SWEEPS)])
    for y in range(TOTAL):
        flat, where = column(last, PAD, rows, y)
        flat[where, :] = flat[where, :] + planes[y][PAD:end, :]
    top = pltpu.make_async_copy(
        last.at[pl.ds(PAD, rows), pl.ds(0, PAD)],
        state_out.at[:, pl.ds(0, PAD)],
        out_sem.at[1],
    )
    top.start()
    displacement, mismatch = solid(1, disp[...])
    part1 = squares(mismatch)
    across = iota((1, width), 1)
    row_of_parts = jnp.where(across == 0, part0, jnp.where(across == 1, part1, 0.0))
    norm_s[...] = jnp.broadcast_to(row_of_parts.reshape(1, 1, width), (n, 1, width))
    exchange(norm_s, norm_r, 5)
    disp[...] = displacement
    moved = pltpu.make_async_copy(disp, disp_out, out_sem.at[2])
    moved.start()

    for copy in ghosts + edges + edges2:
        copy.wait_send()
    finish(req_s, a2a_ss.at[0])
    for k in range(COUPLE):
        finish(wall_s.at[k], a2a_ss.at[1 + 2 * k])
        finish(trac_s.at[k], a2a_ss.at[2 + 2 * k])
    bulk.wait()
    top.wait()
    moved.wait()
    finish(norm_s, a2a_ss.at[5])
    finish(norm_r, a2a_rs.at[5])
    norm_out[...] = jnp.sum(norm_r[...], axis=0)


def store_kernel(state, disp, sums, state_out, disp_out, norm_out, held, moved, added, get, put):
    parts = get.shape[0] - 2
    rows = state.shape[0] // parts
    blocks = [(sums, added, None), (disp, moved, disp_out)]
    for i in range(parts):
        part = pl.ds(i * rows, rows)
        blocks.append((state.at[part], held.at[part], state_out.at[part]))
    arrivals = [
        pltpu.make_async_copy(here, kept, get.at[i]) for i, (here, kept, _) in enumerate(blocks)
    ]
    for copy in arrivals:
        copy.start()
    leaves = []
    for i, (_, kept, there) in enumerate(blocks):
        arrivals[i].wait()
        if there is not None:
            leaves.append(pltpu.make_async_copy(kept, there, put.at[i]))
            leaves[-1].start()
    roots = jnp.sqrt(added[...] + 1e-06)
    across = iota(roots.shape, 1)
    for k in range(COUPLE):
        norm_out[k] = jnp.sum(jnp.where(across == k, roots, 0.0))
    for copy in leaves:
        copy.wait()


def per_device(
    n, dom, fluid_source, coef_ids, coef_table, owner_device, owner_slot,
    solid_init, solid_load, compliance,
):
    rows, depth, width = fluid_source.shape
    solid_rows = solid_init.shape[0]
    tall = rows + 2 * PAD
    f32, bf16 = jnp.float32, jnp.bfloat16
    vmem = pl.BlockSpec(memory_space=pltpu.VMEM)
    smem = pl.BlockSpec(memory_space=pltpu.SMEM)
    hbm = pl.BlockSpec(memory_space=pltpu.HBM)
    block = (COUPLE, n, PAD, width)
    state, disp, sums = (
        pl.pallas_call(
            functools.partial(kernel, n, dom),
            out_shape=(
                jax.ShapeDtypeStruct((rows, depth, width), f32),
                jax.ShapeDtypeStruct((solid_rows, width), f32),
                jax.ShapeDtypeStruct((1, width), f32),
            ),
            in_specs=[hbm] * 8,
            out_specs=(hbm, hbm, vmem),
            scratch_shapes=[
                pltpu.SMEM(coef_table.shape, f32),
                pltpu.VMEM((1, rows), jnp.int32),
                pltpu.VMEM((1, rows), jnp.int32),
                pltpu.VMEM((solid_rows, width), f32),
                pltpu.VMEM((solid_rows, width), f32),
                pltpu.VMEM((width, width), f32),
                pltpu.VMEM((tall, depth, width), f32),
                pltpu.VMEM((tall, depth, width), jnp.int32),
                pltpu.VMEM((tall, depth, width), f32),
                pltpu.VMEM((tall, depth, width), f32),
                pltpu.VMEM((tall, depth, width), f32),
                pltpu.VMEM((TOTAL, tall, width), f32),
                pltpu.VMEM((COUPLE, rows, width), f32),
                pltpu.VMEM((COUPLE, tall, width), f32),
                pltpu.VMEM((SWEEPS, tall, width), f32),
                pltpu.VMEM((rows, width), f32),
                pltpu.VMEM((solid_rows, width), f32),
                pltpu.VMEM((n * PAD, rows), bf16),
                pltpu.VMEM((rows, n * PAD), bf16),
                pltpu.VMEM((n * PAD, solid_rows), bf16),
                pltpu.VMEM((solid_rows, n * PAD), bf16),
                pltpu.VMEM((n, 1, width), jnp.int32),
                pltpu.VMEM((n, 1, width), jnp.int32),
                pltpu.VMEM(block, f32),
                pltpu.VMEM(block, f32),
                pltpu.VMEM(block, f32),
                pltpu.VMEM(block, f32),
                pltpu.VMEM((n, 1, width), f32),
                pltpu.VMEM((n, 1, width), f32),
                pltpu.SemaphoreType.DMA((8,)),
                pltpu.SemaphoreType.DMA((3,)),
                pltpu.SemaphoreType.DMA((2, 2)),
                pltpu.SemaphoreType.DMA((2, 2)),
                pltpu.SemaphoreType.DMA((2 + 2 * COUPLE,)),
                pltpu.SemaphoreType.DMA((2 + 2 * COUPLE,)),
                pltpu.SemaphoreType.DMA((COUPLE, 2)),
                pltpu.SemaphoreType.DMA((COUPLE, 2)),
            ],
            compiler_params=pltpu.CompilerParams(
                collective_id=0, has_side_effects=True, vmem_limit_bytes=VMEM
            ),
        )(
            fluid_source, coef_ids, coef_table,
            owner_device.reshape(1, rows), owner_slot.reshape(1, rows),
            solid_init, solid_load, compliance,
        )
    )
    return tuple(
        pl.pallas_call(
            store_kernel,
            out_shape=(
                jax.ShapeDtypeStruct(state.shape, f32),
                jax.ShapeDtypeStruct(disp.shape, f32),
                jax.ShapeDtypeStruct((COUPLE,), f32),
            ),
            in_specs=[hbm] * 3,
            out_specs=(hbm, hbm, smem),
            scratch_shapes=[
                pltpu.VMEM(state.shape, f32),
                pltpu.VMEM(disp.shape, f32),
                pltpu.VMEM(sums.shape, f32),
                pltpu.SemaphoreType.DMA((10,)),
                pltpu.SemaphoreType.DMA((10,)),
            ],
            compiler_params=pltpu.CompilerParams(vmem_limit_bytes=VMEM),
        )(state, disp, sums)
    )


def solution(mesh):
    rows = P(("sect", "dom"), None)
    cells = P(("sect", "dom"), None, None)
    n = mesh.shape["sect"] * mesh.shape["dom"]
    return jax.shard_map(
        functools.partial(per_device, n, mesh.shape["dom"]),
        mesh=mesh,
        in_specs=(cells, cells, P(), rows, rows, rows, rows, P()),
        out_specs=(cells, rows, P()),
        check_vma=False,
    )
```

```python
import functools

import jax
import jax.numpy as jnp
from jax import lax
from jax.experimental import pallas as pl
from jax.experimental.pallas import tpu as pltpu
from jax.sharding import PartitionSpec as P

SWEEPS = 3
COUPLE = 2
RELAX = 0.5
TOTAL = SWEEPS * COUPLE
GHOST = TOTAL - 1
PAD = 8
STEP = 16
VMEM = 58 * 2**20
MESH = pl.DeviceIdType.MESH


def iota(shape, dim):
    return lax.broadcasted_iota(jnp.int32, shape, dim)


def pieces(x):
    high = x.astype(jnp.bfloat16)
    low = (x - high.astype(jnp.float32)).astype(jnp.bfloat16)
    return high, low


def pick(onehot, x):
    width = x.shape[1]
    both = jnp.concatenate(pieces(x), axis=1)
    out = jnp.dot(onehot, both, preferred_element_type=jnp.float32)
    return out[:, :width] + out[:, width:]


def product(x, y):
    xh, xl = pieces(x)
    yh, yl = pieces(y)
    left = jnp.concatenate([xh, xh, xl], axis=1)
    right = jnp.concatenate([yh, yl, yh], axis=0)
    return jnp.dot(left, right, preferred_element_type=jnp.float32)


def beside(x):
    rows, width = x.shape
    lane = iota(x.shape, 1)
    low = jnp.where(lane == 0, 0.0, pltpu.roll(x, 1, 1))
    high = jnp.where(lane == width - 1, 0.0, pltpu.roll(x, width - 1, 1))
    return low + high


def kernel(
    n, dom, source, ids, table_in, owner_in, slot_in, init_in, load_in, compliance_in,
    state_out, disp_out, norm_out,
    table, owner, slot, init, load, compliance,
    src, idv, inv, even, odd, invp, base, walls, force, trac, disp,
    place, place_t, choose, choose_t,
    req_s, req_r, wall_s, wall_r, trac_s, trac_r, norm_s, norm_r,
    in_sem, out_sem, ghost_ss, ghost_rs, a2a_ss, a2a_rs, edge_ss, edge_rs,
):
    rows, depth, width = source.shape
    end = PAD + rows
    cap = PAD
    sect = n // dom
    my_sect, my_dom = lax.axis_index("sect"), lax.axis_index("dom")
    me = my_sect * dom + my_dom

    def after(sect_at, dom_at):
        over = dom_at + 1 == dom
        dom_next = jnp.where(over, 0, dom_at + 1)
        sect_next = jnp.where(over, sect_at + 1, sect_at)
        return jnp.where(sect_next == sect, 0, sect_next), dom_next

    def ahead(sect_at, dom_at):
        under = dom_at == 0
        dom_next = jnp.where(under, dom - 1, dom_at - 1)
        sect_next = jnp.where(under, sect_at - 1, sect_at)
        return jnp.where(sect_next < 0, sect - 1, sect_next), dom_next

    right = after(my_sect, my_dom)
    left = ahead(my_sect, my_dom)

    def wrapped(value, count):
        return jnp.where(value >= count, value - count, value)

    dom_at = [wrapped(my_dom + step, dom) for step in range(dom)]

    def each_peer(act):
        def one(step, carry):
            sect_at = wrapped(my_sect + step, sect)
            for at in dom_at:
                act(sect_at, at)
            return carry

        lax.fori_loop(1, sect, one, 0)
        for at in dom_at[1:]:
            act(my_sect, at)

    loads = [
        pltpu.make_async_copy(a, b, in_sem.at[i])
        for i, (a, b) in enumerate((
            (owner_in, owner), (slot_in, slot), (table_in, table),
            (ids, idv.at[pl.ds(PAD, rows)]), (source, src.at[pl.ds(PAD, rows)]),
            (init_in, init), (load_in, load), (compliance_in, compliance),
        ))
    ]
    for copy in loads[:2]:
        copy.start()

    barrier = pltpu.get_barrier_semaphore()
    each_peer(lambda *at: pl.semaphore_signal(
        barrier, inc=1, device_id=at, device_id_type=MESH
    ))
    for copy in loads[2:]:
        copy.start()
    for copy in loads[:2]:
        copy.wait()

    owner_row = owner[...]
    slot_row = slot[...]
    hits = (iota((n, rows), 0) == owner_row).astype(jnp.float32)
    before = (iota((rows, rows), 0) < iota((rows, rows), 1)).astype(jnp.bfloat16)
    earlier = jnp.dot(hits.astype(jnp.bfloat16), before, preferred_element_type=jnp.float32)
    rank = jnp.sum(earlier * hits, axis=0, keepdims=True).astype(jnp.int32)
    position = owner_row * cap + rank
    placed = (iota((n * cap, rows), 0) == position).astype(jnp.float32)
    place[...] = placed.astype(jnp.bfloat16)
    wanted = jnp.sum(placed * (slot_row + 1).astype(jnp.float32), axis=1, keepdims=True) - 1.0
    wanted = wanted.reshape(n, cap, 1)
    square = iota((n, cap, width), 2) == iota((n, cap, width), 1)
    req_s[...] = jnp.sum(jnp.where(square, wanted, 0.0), axis=1, keepdims=True).astype(jnp.int32)

    for copy in loads[2:]:
        copy.wait()

    lane = iota((depth, width), 1)
    recip = jnp.zeros((depth, width), jnp.float32)
    for entry in range(table.shape[0]):
        recip = jnp.where(lane == entry, table[entry], recip)
    recip = 1.0 / (6.0 + recip)

    def first(x, scale):
        value = jnp.take_along_axis(recip, idv[x], axis=1, mode="promise_in_bounds")
        if scale is not None:
            value = value * scale
        inv[x] = value
        even[x] = src[x] * value

    def first_block(i, carry):
        for j in range(PAD):
            first(PAD + PAD * i + j, None)
        return carry

    lax.fori_loop(0, rows // PAD, first_block, 0)
    pl.semaphore_wait(barrier, n - 1)

    def exchange(sent, got, phase):
        def one(sect_at, dom_at):
            pltpu.make_async_remote_copy(
                src_ref=sent.at[sect_at * dom + dom_at],
                dst_ref=got.at[me],
                send_sem=a2a_ss.at[phase],
                recv_sem=a2a_rs.at[phase],
                device_id=(sect_at, dom_at),
                device_id_type=MESH,
            ).start()

        each_peer(one)
        got[me] = sent[me]

    def finish(ref, sem):
        part = ref.at[pl.ds(0, n - 1)]
        pltpu.make_async_copy(part, part, sem).wait()

    exchange(req_s, req_r, 0)
    place_t[...] = placed.T.astype(jnp.bfloat16)

    def to_neighbours(from_low, from_high, to_low, to_high, ss, rs):
        copies = [
            pltpu.make_async_remote_copy(
                src_ref=a, dst_ref=b, send_sem=ss(i), recv_sem=rs(i),
                device_id=device, device_id_type=MESH,
            )
            for i, (a, b, device) in enumerate(
                ((from_low, to_high, left), (from_high, to_low, right))
            )
        ]
        for copy in copies:
            copy.start()
        return copies

    ghosts = []
    for number, (whole, held) in enumerate(((source, src), (ids, idv))):
        ghosts += to_neighbours(
            whole.at[pl.ds(0, GHOST)], whole.at[pl.ds(rows - GHOST, GHOST)],
            held.at[pl.ds(PAD - GHOST, GHOST)], held.at[pl.ds(end, GHOST)],
            lambda i: ghost_ss.at[number, i], lambda i: ghost_rs.at[number, i],
        )

    def column(ref, begin, count, y):
        flat = ref.reshape(ref.shape[0] * depth, width)
        return flat, pl.ds(begin * depth + y, count, stride=depth)

    def take(ref, begin, count, y):
        flat, where = column(ref, begin, count, y)
        return flat[where, :]

    low_row = iota((8, width), 0) == 0
    high_row = iota((8, width), 0) == 7

    def sweep(number, begin, stop):
        old, new = (even, odd) if number % 2 == 1 else (odd, even)
        count = stop - begin

        flat = old.reshape(old.shape[0] * depth, width)

        def planes(x, many):
            held = [old[x - 1 + j] for j in range(many + 2)]
            for j in range(many):
                here = held[j + 1]
                at = (x + j) * depth
                up = flat[pl.ds(at - 1, depth), :]
                down = flat[pl.ds(at + 1, depth), :]
                up = jnp.concatenate([jnp.where(low_row, 0.0, up[:8]), up[8:]], axis=0)
                down = jnp.concatenate([down[:-8], jnp.where(high_row, 0.0, down[-8:])], axis=0)
                total = src[x + j] + (held[j] + held[j + 2])
                total = total + (up + down) + beside(here)
                new[x + j] = total * inv[x + j]

        blocks = -(-count // STEP)
        step = -(-count // blocks)

        def block(i, carry):
            planes(jnp.where(i == blocks - 1, stop - step, begin + step * i), step)
            return carry

        if blocks == 1:
            planes(begin, count)
        else:
            lax.fori_loop(0, blocks, block, 0)

    def whole(number):
        sweep(number, PAD - (GHOST - number), end + (GHOST - number))

    def tractions(number):
        new = odd if number % 2 == 1 else even
        base[number // SWEEPS] = take(new, PAD, rows, 0) - take(new, PAD, rows, 1)

    for x in list(range(PAD - GHOST)) + list(range(end + GHOST, end + PAD)):
        inv[x] = jnp.zeros((depth, width), jnp.float32)

    sweep(1, PAD + 1, end - 1)

    finish(req_r, a2a_rs.at[0])
    slots = jnp.sum(jnp.where(square, req_r[...].astype(jnp.float32), 0.0), axis=2, keepdims=True)
    chosen = (iota((n, cap, init.shape[0]), 2).astype(jnp.float32) == slots).astype(jnp.float32)
    chosen = chosen.reshape(n * cap, init.shape[0])
    choose[...] = chosen.astype(jnp.bfloat16)
    wall_s[0] = pick(choose[...], init[...]).reshape(n, cap, width)
    exchange(wall_s.at[0], wall_r.at[0], 1)
    choose_t[...] = chosen.T.astype(jnp.bfloat16)

    for copy in ghosts:
        copy.wait_recv()
    low_scale = jnp.where(me == 0, 0.0, 1.0)
    high_scale = jnp.where(me == n - 1, 0.0, 1.0)
    for x in range(GHOST):
        first(PAD - GHOST + x, low_scale)
        first(end + x, high_scale)
    for y in range(TOTAL):
        invp[y] = take(inv, 0, rows + 2 * PAD, y)

    def wall_of(k):
        finish(wall_r.at[k], a2a_rs.at[1 + 2 * k])
        got = wall_r[k].reshape(n * cap, width)
        mine = pick(place_t[...], got)
        walls[k, PAD:end, :] = mine
        held = walls.at[k]
        return mine, to_neighbours(
            held.at[pl.ds(PAD, PAD)], held.at[pl.ds(rows, PAD)],
            held.at[pl.ds(0, PAD)], held.at[pl.ds(end, PAD)],
            lambda i: edge_ss.at[k, i], lambda i: edge_rs.at[k, i],
        )

    def spread(wall, begun, factor):
        found = {}

        def plane(step, y):
            if y >= len(begun) + step:
                return None
            if step == 0:
                return begun[y]
            if (step, y) not in found:
                terms = [wall] if y == 0 else []
                here = plane(step - 1, y)
                if here is not None:
                    tall = here.shape[0]
                    terms.append(pltpu.roll(here, 1, 0) + pltpu.roll(here, tall - 1, 0))
                    terms.append(beside(here))
                if y > 0:
                    terms.append(plane(step - 1, y - 1))
                terms.append(plane(step - 1, y + 1))
                terms = [term for term in terms if term is not None]
                found[step, y] = functools.reduce(jnp.add, terms) * factor(y)
            return found[step, y]

        return plane

    def iterate(k, begun, meanwhile):
        mine, edges = wall_of(k)
        margin = jnp.zeros((PAD, width), jnp.float32)
        own = spread(jnp.concatenate([margin, mine, margin], axis=0), begun, lambda y: invp[y])
        trac[...] = (own(SWEEPS, 0) - own(SWEEPS, 1))[PAD:end, :]
        meanwhile()
        trac[...] = trac[...] + base[k]
        for copy in edges:
            copy.wait_recv()

        outer = jnp.concatenate(
            [walls[k, :PAD, :], margin, margin, walls[k, end:, :]], axis=0
        )
        other = spread(outer, [], lambda y: jnp.concatenate(
            [invp[y, :2 * PAD, :], invp[y, end - PAD:, :]], axis=0
        ))
        jump = other(SWEEPS, 0) - other(SWEEPS, 1)
        trac[:PAD, :] = trac[:PAD, :] + jump[PAD:2 * PAD, :]
        trac[rows - PAD:, :] = trac[rows - PAD:, :] + jump[2 * PAD:3 * PAD, :]
        trac_s[k] = pick(place[...], trac[...]).reshape(n, cap, width)
        exchange(trac_s.at[k], trac_r.at[k], 2 + 2 * k)
        middle = jnp.zeros((rows - 2 * PAD, width), jnp.float32)
        planes = []
        for y in range(len(begun) + SWEEPS):
            total = own(SWEEPS, y)
            if y < SWEEPS:
                share = other(SWEEPS, y)
                total = total + jnp.concatenate(
                    [share[:2 * PAD, :], middle, share[2 * PAD:, :]], axis=0
                )
            planes.append(total)
        return planes, edges

    def solid(k, displacement):
        finish(trac_r.at[k], a2a_rs.at[2 + 2 * k])
        got = trac_r[k].reshape(n * cap, width)
        total = load[...] + pick(choose_t[...], got)
        mismatch = product(total, compliance[...]) - displacement
        return displacement + RELAX * mismatch, mismatch

    def squares(mismatch):
        return jnp.sum(jnp.sum(mismatch * mismatch, axis=0, keepdims=True), axis=1, keepdims=True)

    sweep(1, PAD - GHOST + 1, PAD + 1)
    sweep(1, end - 1, end + GHOST - 1)
    half = PAD + rows // 2
    sweep(2, PAD - GHOST + 2, half)

    def rest_of_2():
        sweep(2, half, end + GHOST - 2)
        tractions(2)

    planes, edges = iterate(0, [], rest_of_2)
    for y in range(SWEEPS):
        force[y] = planes[y]
    whole(3)
    sweep(4, PAD - 1, half)
    displacement, mismatch = solid(0, init[...])
    wall_s[1] = pick(choose[...], displacement).reshape(n, cap, width)
    exchange(wall_s.at[1], wall_r.at[1], 3)
    disp[...] = displacement
    part0 = squares(mismatch)
    sweep(4, half, end + 1)
    sweep(5, PAD, half)
    last = odd if GHOST % 2 == 1 else even
    bulk = pltpu.make_async_copy(
        last.at[pl.ds(PAD, rows), pl.ds(PAD, depth - PAD)],
        state_out.at[:, pl.ds(PAD, depth - PAD)],
        out_sem.at[0],
    )

    def rest_of_5():
        sweep(5, half, end)
        tractions(5)
        bulk.start()

    planes, edges2 = iterate(1, [force[y] for y in range(SWEEPS)], rest_of_5)
    for y in range(TOTAL):
        flat, where = column(last, PAD, rows, y)
        flat[where, :] = flat[where, :] + planes[y][PAD:end, :]
    top = pltpu.make_async_copy(
        last.at[pl.ds(PAD, rows), pl.ds(0, PAD)],
        state_out.at[:, pl.ds(0, PAD)],
        out_sem.at[1],
    )
    top.start()
    displacement, mismatch = solid(1, disp[...])
    part1 = squares(mismatch)
    across = iota((1, width), 1)
    row_of_parts = jnp.where(across == 0, part0, jnp.where(across == 1, part1, 0.0))
    norm_s[...] = jnp.broadcast_to(row_of_parts.reshape(1, 1, width), (n, 1, width))
    exchange(norm_s, norm_r, 5)
    disp[...] = displacement
    moved = pltpu.make_async_copy(disp, disp_out, out_sem.at[2])
    moved.start()

    for copy in ghosts + edges + edges2:
        copy.wait_send()
    finish(req_s, a2a_ss.at[0])
    for k in range(COUPLE):
        finish(wall_s.at[k], a2a_ss.at[1 + 2 * k])
        finish(trac_s.at[k], a2a_ss.at[2 + 2 * k])
    bulk.wait()
    top.wait()
    moved.wait()
    finish(norm_s, a2a_ss.at[5])
    finish(norm_r, a2a_rs.at[5])
    norm_out[...] = jnp.sum(norm_r[...], axis=0)


def store_kernel(state, disp, sums, state_out, disp_out, norm_out, held, moved, added, get, put):
    parts = get.shape[0] - 2
    rows = state.shape[0] // parts
    blocks = [(sums, added, None), (disp, moved, disp_out)]
    for i in range(parts):
        part = pl.ds(i * rows, rows)
        blocks.append((state.at[part], held.at[part], state_out.at[part]))
    arrivals = [
        pltpu.make_async_copy(here, kept, get.at[i]) for i, (here, kept, _) in enumerate(blocks)
    ]
    for copy in arrivals:
        copy.start()
    leaves = []
    for i, (_, kept, there) in enumerate(blocks):
        arrivals[i].wait()
        if there is not None:
            leaves.append(pltpu.make_async_copy(kept, there, put.at[i]))
            leaves[-1].start()
    roots = jnp.sqrt(added[...] + 1e-06)
    across = iota(roots.shape, 1)
    for k in range(COUPLE):
        norm_out[k] = jnp.sum(jnp.where(across == k, roots, 0.0))
    for copy in leaves:
        copy.wait()


def per_device(
    n, dom, fluid_source, coef_ids, coef_table, owner_device, owner_slot,
    solid_init, solid_load, compliance,
):
    rows, depth, width = fluid_source.shape
    solid_rows = solid_init.shape[0]
    tall = rows + 2 * PAD
    f32, bf16 = jnp.float32, jnp.bfloat16
    vmem = pl.BlockSpec(memory_space=pltpu.VMEM)
    smem = pl.BlockSpec(memory_space=pltpu.SMEM)
    hbm = pl.BlockSpec(memory_space=pltpu.HBM)
    block = (COUPLE, n, PAD, width)
    state, disp, sums = (
        pl.pallas_call(
            functools.partial(kernel, n, dom),
            out_shape=(
                jax.ShapeDtypeStruct((rows, depth, width), f32),
                jax.ShapeDtypeStruct((solid_rows, width), f32),
                jax.ShapeDtypeStruct((1, width), f32),
            ),
            in_specs=[hbm] * 8,
            out_specs=(hbm, hbm, vmem),
            scratch_shapes=[
                pltpu.SMEM(coef_table.shape, f32),
                pltpu.VMEM((1, rows), jnp.int32),
                pltpu.VMEM((1, rows), jnp.int32),
                pltpu.VMEM((solid_rows, width), f32),
                pltpu.VMEM((solid_rows, width), f32),
                pltpu.VMEM((width, width), f32),
                pltpu.VMEM((tall, depth, width), f32),
                pltpu.VMEM((tall, depth, width), jnp.int32),
                pltpu.VMEM((tall, depth, width), f32),
                pltpu.VMEM((tall, depth, width), f32),
                pltpu.VMEM((tall, depth, width), f32),
                pltpu.VMEM((TOTAL, tall, width), f32),
                pltpu.VMEM((COUPLE, rows, width), f32),
                pltpu.VMEM((COUPLE, tall, width), f32),
                pltpu.VMEM((SWEEPS, tall, width), f32),
                pltpu.VMEM((rows, width), f32),
                pltpu.VMEM((solid_rows, width), f32),
                pltpu.VMEM((n * PAD, rows), bf16),
                pltpu.VMEM((rows, n * PAD), bf16),
                pltpu.VMEM((n * PAD, solid_rows), bf16),
                pltpu.VMEM((solid_rows, n * PAD), bf16),
                pltpu.VMEM((n, 1, width), jnp.int32),
                pltpu.VMEM((n, 1, width), jnp.int32),
                pltpu.VMEM(block, f32),
                pltpu.VMEM(block, f32),
                pltpu.VMEM(block, f32),
                pltpu.VMEM(block, f32),
                pltpu.VMEM((n, 1, width), f32),
                pltpu.VMEM((n, 1, width), f32),
                pltpu.SemaphoreType.DMA((8,)),
                pltpu.SemaphoreType.DMA((3,)),
                pltpu.SemaphoreType.DMA((2, 2)),
                pltpu.SemaphoreType.DMA((2, 2)),
                pltpu.SemaphoreType.DMA((2 + 2 * COUPLE,)),
                pltpu.SemaphoreType.DMA((2 + 2 * COUPLE,)),
                pltpu.SemaphoreType.DMA((COUPLE, 2)),
                pltpu.SemaphoreType.DMA((COUPLE, 2)),
            ],
            compiler_params=pltpu.CompilerParams(
                collective_id=0, has_side_effects=True, vmem_limit_bytes=VMEM
            ),
        )(
            fluid_source, coef_ids, coef_table,
            owner_device.reshape(1, rows), owner_slot.reshape(1, rows),
            solid_init, solid_load, compliance,
        )
    )
    return tuple(
        pl.pallas_call(
            store_kernel,
            out_shape=(
                jax.ShapeDtypeStruct(state.shape, f32),
                jax.ShapeDtypeStruct(disp.shape, f32),
                jax.ShapeDtypeStruct((COUPLE,), f32),
            ),
            in_specs=[hbm] * 3,
            out_specs=(hbm, hbm, smem),
            scratch_shapes=[
                pltpu.VMEM(state.shape, f32),
                pltpu.VMEM(disp.shape, f32),
                pltpu.VMEM(sums.shape, f32),
                pltpu.SemaphoreType.DMA((10,)),
                pltpu.SemaphoreType.DMA((10,)),
            ],
            compiler_params=pltpu.CompilerParams(vmem_limit_bytes=VMEM),
        )(state, disp, sums)
    )


def solution(mesh):
    rows = P(("sect", "dom"), None)
    cells = P(("sect", "dom"), None, None)
    n = mesh.shape["sect"] * mesh.shape["dom"]
    return jax.shard_map(
        functools.partial(per_device, n, mesh.shape["dom"]),
        mesh=mesh,
        in_specs=(cells, cells, P(), rows, rows, rows, rows, P()),
        out_specs=(cells, rows, P()),
        check_vma=False,
    )
```
